512 devices in a mesh: group: 32 (over z, y_lo), sample: 16 (over y_hi, x, core).
Axes of the slice: x: 4, y: 4 (y_hi: 2, y_lo: 2; y = y_hi * 2 + y_lo), z: 16, core: 2. Of those that a mesh axis runs over, the one named last changes fastest.
Arguments:
- trainer_flat: bfloat16 [512, 6480], P(('group', 'sample')), may hold values from -0.109375 to 0.109375
- matching: int32 [512], replicated, may hold values from 0 to 511, each once
- prefix_kv: bfloat16 [32, 8192, 128], P('group', 'sample'), may hold values from -500 to 500
- prefix_blocks: int32 [32], P('group'), may hold values from 1 to 64, as said below
- inputs: bfloat16 [4, 32, 128, 2880], P(None, 'group', 'sample'), may hold values from -6 to 6
Outputs:
- attended: bfloat16 [4, 32, 128, 2880], P(None, 'group', 'sample')
The draws below stay inside these ranges and needn't reach their ends.
Inputs may be any that keep to these rules, and one draw needn't show every extreme that they name: `prefix_blocks`: some prompt's prefix fills all 8192 positions in every draw.
All inputs are finite; a program needn't handle non-finite values.
Results may differ from the reference program's by a relative error of at most 0.025.
Values may be sent and summed in bfloat16 or wider, within the bound.
No kernel may reach another device: no remote copies, remote signals or barrier semaphores. Data moves between devices by JAX's collectives and lax.ppermute only.
A program may use at most 64 MiB of HBM per device.

```python
import math
import jax
import jax.numpy as jnp
from jax import lax

D = 2880
HEAD = 64
QHEADS = 8
STEPS = 4
TILES = 512
GROUPS = 32
SAMPLES = 128
PREFIX = 8192
FLAT = 3317760


def loud_prompt(key):
    return jax.random.randint(jax.random.fold_in(key, 5), (), 0, GROUPS)


def draw_prefix_blocks(key, part):
    chosen = loud_prompt(key)
    key = jax.random.fold_in(key, 7)
    most = PREFIX // 128
    drawn = jax.random.randint(key, (GROUPS,), 1, most + 1)
    return jnp.where(jnp.arange(GROUPS) == chosen, most, drawn).astype(jnp.int32)


def draw_prefix_kv(key, part):
    chosen = loud_prompt(key)
    key = jax.random.fold_in(key, 9)
    subkeys = jax.random.split(key, 6)
    layout = (GROUPS, PREFIX, 2 * HEAD)
    base = jax.random.truncated_normal(subkeys[0], -4.0, 4.0, layout, jnp.float32)
    spread = jnp.exp(jax.random.uniform(subkeys[1], (GROUPS, PREFIX, 1), jnp.float32, -0.7, 0.7))
    base = base * spread
    strength = jnp.exp(jax.random.uniform(subkeys[3], (GROUPS, 1, 1), jnp.float32, math.log(0.4), math.log(60.0)))
    strength = jnp.where(jnp.arange(GROUPS)[:, None, None] == chosen, 60.0, strength)
    position = jnp.arange(PREFIX)[None, :, None]
    paired = (jax.random.uniform(subkeys[4], (GROUPS, PREFIX, 1), jnp.float32) < 0.25) & (position % 2 == 1)
    stretch = jax.random.uniform(subkeys[5], (GROUPS, PREFIX, 1), jnp.float32, 1.004, 1.012)
    key_part = base[..., :HEAD]
    key_part = jnp.where(paired, jnp.roll(key_part, 1, axis=1) * stretch, key_part) * strength
    return jnp.concatenate([key_part, base[..., HEAD:]], -1).astype(jnp.bfloat16)


def block_levels(rng, extent, cuts, low, largest):
    def one(dim, blocks):
        heights = jax.random.uniform(jax.random.fold_in(jax.random.fold_in(rng, 6), dim), (blocks,), jnp.float32, low / len(cuts), largest / len(cuts))
        return jnp.repeat(jnp.exp(heights), extent[dim] // blocks).reshape((-1,) + (1,) * (len(extent) - dim - 1))

    level = one(*cuts[0])
    for cut in cuts[1:]:
        level = level * one(*cut)
    return level


def noise(rng, shape, deviation, limit, pieces=(), kind=jnp.bfloat16):
    entries = jax.random.normal(rng, shape, jnp.float32) * deviation
    if len(pieces) > 0:
        entries = block_levels(rng, shape, pieces, -0.22, 0.18) * entries
    return jnp.clip(entries, min=-limit, max=limit).astype(kind)


def setup_inputs(seed: int = 0) -> dict:
    key_list = jax.random.split(jax.random.key(seed), 6)
    trainer_flat = noise(key_list[0], (TILES, FLAT // TILES), D ** -0.5, 0.109375, ((0, 512),))
    matching = jax.random.permutation(key_list[1], TILES).astype(jnp.int32)
    prefix_kv = draw_prefix_kv(jax.random.fold_in(key_list[5], 71), 0)
    prefix_blocks = draw_prefix_blocks(jax.random.fold_in(key_list[5], 71), 0)
    inputs = noise(key_list[4], (STEPS, GROUPS, SAMPLES, D), 1.0, 6.0, ((1, 32), (2, 16)))
    return {"trainer_flat": trainer_flat, "matching": matching, "prefix_kv": prefix_kv, "prefix_blocks": prefix_blocks, "inputs": inputs}


def one_group(weight_in, weight_out, prefix_group, blocks, inputs_group):
    scale = HEAD ** -0.5
    query_width = QHEADS * HEAD
    keys = prefix_group[:, :HEAD].astype(jnp.float32)
    values = prefix_group[:, HEAD:].astype(jnp.float32)
    valid = jnp.arange(PREFIX, dtype=jnp.int32) < blocks * 128
    own_key_list = []
    own_value_list = []
    results = []
    for step in range(STEPS):
        projected = jnp.dot(inputs_group[step], weight_in, preferred_element_type=jnp.float32)
        query = projected[:, :query_width].astype(jnp.bfloat16).reshape(SAMPLES, QHEADS, HEAD).astype(jnp.float32)
        own_key_list.append(projected[:, query_width:query_width + HEAD].astype(jnp.bfloat16).astype(jnp.float32))
        own_value_list.append(projected[:, query_width + HEAD:].astype(jnp.bfloat16).astype(jnp.float32))
        keys_own = jnp.stack(own_key_list, 1)
        values_own = jnp.stack(own_value_list, 1)
        prefix_scores = jnp.einsum('shd,kd->shk', query, keys) * scale
        prefix_scores = jnp.where(valid, prefix_scores, jnp.float32(-1e30))
        own_scores = jnp.einsum('shd,sjd->shj', query, keys_own) * scale
        top = jnp.maximum(jnp.max(prefix_scores, -1), jnp.max(own_scores, -1))[..., None]
        prefix_weights = jnp.where(valid, jnp.exp(prefix_scores - top), 0.0).astype(jnp.bfloat16).astype(jnp.float32)
        own_weights = jnp.exp(own_scores - top).astype(jnp.bfloat16).astype(jnp.float32)
        total = jnp.sum(prefix_weights, -1) + jnp.sum(own_weights, -1)
        summed = jnp.einsum('shk,kd->shd', prefix_weights, values) + jnp.einsum('shj,sjd->shd', own_weights, values_own)
        attended_rows = (summed / total[..., None]).astype(jnp.bfloat16).reshape(SAMPLES, query_width)
        results.append(jnp.dot(attended_rows, weight_out, preferred_element_type=jnp.float32).astype(jnp.bfloat16))
    return jnp.stack(results, 0)


def reference(trainer_flat, matching, prefix_kv, prefix_blocks, inputs):
    full = jnp.zeros_like(trainer_flat).at[matching].set(trainer_flat).reshape(-1)
    width_in = QHEADS * HEAD + 2 * HEAD
    weight_in = full[:D * width_in].reshape(D, width_in)
    weight_out = full[D * width_in:].reshape(QHEADS * HEAD, D)
    inputs_all = jnp.transpose(inputs, (1, 0, 2, 3))
    outputs = lax.map(lambda item: one_group(weight_in, weight_out, item[0], item[1], item[2]), (prefix_kv, prefix_blocks, inputs_all))
    return jnp.transpose(outputs, (1, 0, 2, 3))
```

```python
import functools

import jax
import jax.numpy as jnp
import numpy as np
from jax import lax
from jax.experimental import pallas as pl
from jax.experimental.pallas import tpu as pltpu
from jax.sharding import PartitionSpec as P

D = 2880
HEAD = 64
QHEADS = 8
AXES = ("group", "sample")
TILE = 6480
IN_ROWS = 2880
IN_SIZE = 2880 * 640
SLOT = 56
USED = 55
ROWS = 32
VMEM = pl.BlockSpec(memory_space=pltpu.VMEM)
SMEM = pl.BlockSpec(memory_space=pltpu.SMEM)
MIB = 1024 * 1024


def device_id(z, y, x, core):
    return z * 32 + (y % 2) * 16 + (y // 2) * 8 + x * 2 + core


Z_GROUPS = [
    [device_id(z, y, x, c) for z in range(16)] for y in range(4) for x in range(4) for c in range(2)
]


def line_groups(x_core):
    along_x = [[device_id(z, y, x, x_core) for x in range(4)] for z in range(16) for y in range(4)]
    along_y = [
        [device_id(z, y, x, 1 - x_core) for y in range(4)] for z in range(16) for x in range(4)
    ]
    return along_x + along_y


def moves(step):
    pairs = []
    for z in range(16):
        for y in range(4):
            for x in range(4):
                for c in range(2):
                    y2, x2, c2 = step(y, x, c)
                    pairs.append((device_id(z, y, x, c), device_id(z, y2 % 4, x2 % 4, c2)))
    return pairs


CORE_SWAP = moves(lambda y, x, c: (y, x, 1 - c))
X_UP = moves(lambda y, x, c: (y, x + 1, c))
X_DOWN = moves(lambda y, x, c: (y, x - 1, c))
Y_FAR = moves(lambda y, x, c: (y + 2, x, c))
RING_UP = moves(lambda y, x, c: (y, x + 1, c) if c else (y + 1, x, c))
RING_DOWN = moves(lambda y, x, c: (y, x - 1, c) if c else (y - 1, x, c))


def form_kernel(matching_ref, tile_ref, out_ref, buf_ref):
    me = lax.axis_index("group") * 16 + lax.axis_index("sample")
    place = matching_ref[me]
    buf_ref[...] = jnp.zeros((64, 128), jnp.float32)
    for r in range(50):
        buf_ref[r : r + 1, :] = tile_ref[:, 128 * r : 128 * r + 128].astype(jnp.float32)
    buf_ref[50:51, :80] = tile_ref[:, 6400:6480].astype(jnp.float32)
    raw = buf_ref[...]
    row = lax.broadcasted_iota(jnp.int32, (64, 128), 0)
    lane = lax.broadcasted_iota(jnp.int32, (64, 128), 1)
    in_len = jnp.clip(IN_SIZE - TILE * place, 0, TILE)
    part = jnp.where(row * 128 + lane < in_len, raw, 0.0)
    shift = 80 * (place & 7)
    lanes = shift & 127
    turned = pltpu.roll(part, lanes, 1)
    above = pltpu.roll(turned, 1, 0)
    shifted = pltpu.roll(jnp.where(lane >= lanes, turned, above), shift >> 7, 0)
    units = []
    lane8 = lax.broadcasted_iota(jnp.int32, (8, 128), 1)
    row8 = lax.broadcasted_iota(jnp.int32, (8, 128), 0)
    for i in range(9):
        base, off = divmod(720 * i, 128)
        window = buf_ref[base : base + 8, :]
        if off:
            window = pltpu.roll(window, 128 - off, 1)
            below = pltpu.roll(window, 7, 0)
            window = jnp.where(lane8 < 128 - off, window, below)
        units.append(jnp.where((row8 < 5) | (lane8 < 80), window, 0.0)[:6])
    for i in range(9):
        buf_ref[1 + 6 * i : 7 + 6 * i, :] = units[i]
    first = 1 + 6 * jnp.clip(2560 - 9 * place, 0, 9)
    out = jnp.where((row >= first) & (row < 55), buf_ref[...], 0.0) + shifted
    out = out[:SLOT].astype(jnp.bfloat16)
    for j in range(out_ref.shape[0]):
        out_ref[j] = out


def merge_kernel(in_ref, out_ref, buf_ref):
    for j in range(16):
        buf_ref[SLOT * j : SLOT * j + SLOT, :] = in_ref[j].astype(jnp.float32)
    for r in range(USED):
        low = buf_ref[pl.ds(r, 8, stride=SLOT), :]
        high = buf_ref[pl.ds(r + 8 * SLOT, 8, stride=SLOT), :]
        both = jnp.concatenate([low, high], 0).astype(jnp.bfloat16)
        for k in range(out_ref.shape[0]):
            out_ref[k, r] = both


def read_weights(refs, rows):
    columns = []
    for r in rows:
        columns.append(jnp.concatenate([ref[:, r].reshape(-1, 128) for ref in refs], 0))
    return jnp.concatenate(columns, 1)


def chip_place():
    group, sample = lax.axis_index("group"), lax.axis_index("sample")
    core = sample & 1
    x = (sample >> 1) & 3
    y = (sample >> 3) * 2 + (group & 1)
    return y, x, core


def ring_offset(piece):
    return jnp.where(piece == 0, 0, jnp.where(piece == 1, 3, piece - 1))


def slot_places(matching_row):
    y0, x0, core0 = chip_place()
    slot = lax.broadcasted_iota(jnp.int32, (1, 512), 1)
    core = core0 ^ (slot >> 8)
    offset = ring_offset((slot >> 6) & 3)
    line = (slot >> 4) & 3
    y = jnp.where(core == 0, (y0 + offset) & 3, line)
    x = jnp.where(core == 0, line, (x0 + offset) & 3)
    device = (slot & 15) * 32 + (y & 1) * 16 + (y >> 1) * 8 + x * 2 + core
    rows = lax.broadcasted_iota(jnp.int32, (512, 512), 0)
    chosen = jnp.where(rows == device, 1.0, 0.0).astype(jnp.bfloat16)
    row = lax.broadcasted_iota(jnp.int32, (8, 512), 0)
    digits = jnp.where(row == 0, matching_row >> 4, jnp.where(row == 1, matching_row & 15, 0))
    picked = jnp.dot(
        digits.astype(jnp.float32).astype(jnp.bfloat16), chosen, preferred_element_type=jnp.float32
    ).astype(jnp.int32)
    return picked[0:1] * 16 + picked[1:2]


def pick_kernel(x_ref, matching_ref, xg_ref, place_ref, xs_ref, a_ref):
    place = slot_places(matching_ref[...])
    place_ref[...] = place
    xs_ref[:, 2816:] = jnp.zeros((ROWS, 256), jnp.float32)
    xs_ref[:, :D] = x_ref[...].astype(jnp.float32).reshape(ROWS, D)
    xs = xs_ref[...]
    for i in range(11):
        moved = xs if i == 0 else pltpu.roll(xs, 3072 - i, 1)
        a_ref[ROWS * i : ROWS * i + ROWS, :] = moved.astype(jnp.bfloat16)
    start = jnp.where(place <= 284, 10 * place + (place >> 3), -1)
    total = None
    for k in range(12):
        rows = lax.broadcasted_iota(jnp.int32, (256, 512), 0) + 256 * k
        chosen = jnp.where(rows == start, 1.0, 0.0).astype(jnp.bfloat16)
        term = jnp.dot(
            a_ref[:, 256 * k : 256 * k + 256], chosen, preferred_element_type=jnp.float32
        )
        total = term if total is None else total + term
    xg_ref[...] = total.astype(jnp.bfloat16)


def project(xg_ref, halves):
    blocks = []
    for cols in ((0, 1), (2, 3), (4,)):
        total = None
        for half in range(2):
            for i in range(11):
                term = jnp.dot(
                    xg_ref[ROWS * i : ROWS * i + ROWS, 256 * half : 256 * half + 256],
                    read_weights(halves[half], [5 * i + b for b in cols]),
                    preferred_element_type=jnp.float32,
                )
                total = term if total is None else total + term
        blocks.append(total)
    return jnp.concatenate(blocks, 1)


CHUNK = 1024
SHARD = 512


def tail_kernel(
    limit_ref, xg_ref, place_ref, m0, m1, m2, m3, m4, o0, o1, o2, o3, o4, near_ref, far_ref, out_ref,
    s_ref, w_ref, og_ref, acc_ref,
):
    halves = ((m0, m1, m2, m3, m4), (o0, o1, o2, o3, o4))
    projected = project(xg_ref, halves)
    y0, x0, core0 = chip_place()
    rounded = projected.astype(jnp.bfloat16)
    own_kv = rounded[:, 512:640]
    heads = []
    zero = jnp.zeros((ROWS, HEAD), jnp.float32)
    for h in range(QHEADS):
        heads.append(jnp.concatenate([projected[:, HEAD * h : HEAD * h + HEAD], zero], 1))
    query = jnp.concatenate(heads, 0).astype(jnp.bfloat16)
    count = QHEADS * ROWS
    scale = np.float32(HEAD**-0.5 * np.log2(np.e))
    contract = (((1,), (1,)), ((), ()))
    limit = limit_ref[0] * 128

    own = lax.dot_general(query, own_kv, contract, preferred_element_type=jnp.float32)
    row = lax.broadcasted_iota(jnp.int32, (count, ROWS), 0)
    col = lax.broadcasted_iota(jnp.int32, (count, ROWS), 1)
    allowed = ((row & 7) == (col & 7)) & ((col >> 3) <= ((row >> 3) & 3))
    own = jnp.where(allowed, own, -1e30)

    chunks = 16 * SHARD // CHUNK
    def read_keys(k):
        ref = near_ref if k < chunks // 2 else far_ref
        first = CHUNK * (k % (chunks // 2))
        return ref[first : first + CHUNK, :]

    peak = jnp.full((count, 128), -1e30, jnp.float32)
    for k in range(chunks):
        scores = lax.dot_general(
            query, read_keys(k), contract, preferred_element_type=jnp.float32
        )
        bias = []
        for n in range(CHUNK // SHARD * k, CHUNK // SHARD * (k + 1)):
            x = (x0 + (0, 3, 1, 2)[n & 3]) & 3
            shard = ((y0 >> 1) ^ ((n >> 2) & 1)) * 8 + x * 2 + (core0 ^ (n >> 3))
            keys = lax.broadcasted_iota(jnp.int32, (1, SHARD), 1)
            bias.append(jnp.where(keys < limit - SHARD * shard, 0.0, -1e30))
        scores = scores + jnp.concatenate(bias, 1)
        s_ref[:, CHUNK * k : CHUNK * k + CHUNK] = scores
        for n in range(CHUNK // 128):
            peak = jnp.maximum(peak, scores[:, 128 * n : 128 * n + 128])
    top = jnp.maximum(jnp.max(peak, 1, keepdims=True), jnp.max(own, 1, keepdims=True))
    floor = top * scale

    ones = jnp.float32(1)

    def with_ones(piece):
        lane = lax.broadcasted_iota(jnp.int32, piece.shape, 1)
        return jnp.where(lane < HEAD, ones, piece.astype(jnp.float32)).astype(jnp.bfloat16)

    weights = jnp.where(allowed, jnp.exp2(own * scale - floor), 0.0).astype(jnp.bfloat16)
    summed = jnp.dot(weights, with_ones(own_kv), preferred_element_type=jnp.float32)
    for k in range(chunks):
        weights = jnp.exp2(s_ref[:, CHUNK * k : CHUNK * k + CHUNK] * scale - floor)
        summed = summed + jnp.dot(
            weights.astype(jnp.bfloat16),
            with_ones(read_keys(k)),
            preferred_element_type=jnp.float32,
        )
    mixed = summed[:, HEAD:] / summed[:, :HEAD]
    og_ref[...] = jnp.zeros(og_ref.shape, jnp.float32)
    for h in range(QHEADS):
        og_ref[:, 128 + HEAD * h : 128 + HEAD * h + HEAD] = mixed[ROWS * h : ROWS * h + ROWS]

    place = place_ref[...]
    unit = 9 * place - 2560
    base = (unit >> 2) + 1
    shown = jnp.where(place >= 284, base, -1)
    padded = og_ref[...]
    moved = [
        pltpu.roll(padded, 1, 1)[:, 128:640],
        padded[:, 128:640],
        pltpu.roll(padded, 767, 1)[:, 128:640],
    ]
    stacked = jnp.concatenate(moved, 0).astype(jnp.bfloat16)
    chosen = jnp.where(
        lax.broadcasted_iota(jnp.int32, (512, 512), 0) == shown, 1.0, 0.0
    ).astype(jnp.bfloat16)
    picked = jnp.dot(stacked, chosen, preferred_element_type=jnp.float32)
    phase = unit & 3
    for i in range(9):
        for c in range(4):
            wanted = (c - i) % 4
            d = (wanted + i) // 4
            w_ref[ROWS * c : ROWS * c + ROWS, 512 * i : 512 * i + 512] = jnp.where(
                phase == wanted, picked[ROWS * d : ROWS * d + ROWS], 0.0
            ).astype(jnp.bfloat16)
    acc_ref[...] = jnp.zeros(acc_ref.shape, jnp.float32)
    sides = []
    for cols in ((0, 1), (2, 3), (4, 5)):
        total = None
        for i in range(9):
            for half in range(2):
                term = jnp.dot(
                    w_ref[:, 512 * i + 256 * half : 512 * i + 256 * half + 256],
                    read_weights(halves[half], [1 + 6 * i + b for b in cols]),
                    preferred_element_type=jnp.float32,
                )
                total = term if total is None else total + term
        sides.append(total)
    sides.append(jnp.zeros((4 * ROWS, 128), jnp.float32))
    wide = jnp.concatenate(sides, 1)
    for c in range(4):
        first, off = divmod(720 * c, 128)
        block = wide[ROWS * c : ROWS * c + ROWS]
        if off:
            block = pltpu.roll(block, off, 1)
        span = pl.ds(128 * first, 896)
        acc_ref[:, span] = acc_ref[:, span] + block
    out_ref[...] = acc_ref[:, :D].reshape(out_ref.shape).astype(jnp.bfloat16)


def shards(trainer_flat, matching, prefix_kv, prefix_blocks, inputs):
    bf16, f32 = jnp.bfloat16, jnp.float32
    core = lax.axis_index("sample") % 2
    by_place = matching.reshape(16, 2, 2, 4, 2)
    half0 = by_place[..., 0].transpose(2, 1, 3, 0).reshape(1, 256)
    half1 = by_place[..., 1].transpose(3, 2, 1, 0).reshape(1, 256)
    places = jnp.where(
        core == 0, jnp.concatenate([half0, half1], 1), jnp.concatenate([half1, half0], 1)
    )
    x = inputs[:, 0]
    x = inputs[:, 0]
    prefix = prefix_kv[0]
    below = lax.ppermute(prefix, AXES, X_UP)
    above = lax.ppermute(prefix, AXES, X_DOWN)
    across = lax.ppermute(below, AXES, X_UP)
    line_keys = lax.concatenate([prefix, below, above, across], 0)
    far_keys = lax.ppermute(line_keys, AXES, Y_FAR)
    core_keys = lax.concatenate([line_keys, far_keys], 0)
    other_keys = lax.ppermute(core_keys, AXES, CORE_SWAP)

    formed = pl.pallas_call(
        form_kernel,
        out_shape=jax.ShapeDtypeStruct((16, SLOT, 128), bf16),
        in_specs=[SMEM, VMEM],
        out_specs=VMEM,
        scratch_shapes=[pltpu.VMEM((64, 128), f32)],
        name="form",
    )(matching, trainer_flat)
    along_z = lax.all_to_all(formed, AXES, 0, 0, tiled=True, axis_index_groups=Z_GROUPS)
    merged = pl.pallas_call(
        merge_kernel,
        out_shape=jax.ShapeDtypeStruct((4, USED, 16, 128), bf16),
        in_specs=[VMEM],
        out_specs=VMEM,
        scratch_shapes=[pltpu.VMEM((16 * SLOT, 128), f32)],
        name="merge",
    )(along_z)
    lines = lax.all_to_all(merged, AXES, 0, 0, tiled=True, axis_index_groups=line_groups(0))
    low = lax.ppermute(lines, AXES, RING_UP)
    high = lax.ppermute(lines, AXES, RING_DOWN)
    end0 = lax.ppermute(low[:2], AXES, RING_UP)
    end1 = lax.ppermute(high[2:], AXES, RING_DOWN)
    mine = [lines, low, high, end0, end1]
    other = [lax.ppermute(piece, AXES, CORE_SWAP) for piece in mine]
    gathered, places = pl.pallas_call(
        pick_kernel,
        out_shape=(
            jax.ShapeDtypeStruct((11 * ROWS, 512), bf16),
            jax.ShapeDtypeStruct((1, 512), jnp.int32),
        ),
        in_specs=[VMEM] * 2,
        out_specs=(VMEM, VMEM),
        scratch_shapes=[pltpu.VMEM((ROWS, 3072), f32), pltpu.VMEM((11 * ROWS, 3072), bf16)],
        compiler_params=pltpu.CompilerParams(vmem_limit_bytes=40 * MIB),
        name="pick",
    )(x, matching.reshape(1, 512))
    output = pl.pallas_call(
        tail_kernel,
        out_shape=jax.ShapeDtypeStruct(x.shape, bf16),
        in_specs=[SMEM] + [VMEM] * 14,
        out_specs=VMEM,
        scratch_shapes=[
            pltpu.VMEM((QHEADS * ROWS, 16 * SHARD), f32),
            pltpu.VMEM((4 * ROWS, 9 * 512), bf16),
            pltpu.VMEM((ROWS, 768), f32),
            pltpu.VMEM((ROWS, 3072), f32),
        ],
        compiler_params=pltpu.CompilerParams(vmem_limit_bytes=50 * MIB),
        name="tail",
    )(prefix_blocks, gathered, places, *mine, *other, core_keys, other_keys)
    return output[:, None]


def solution(mesh):
    in_specs = (
        P(("group", "sample"), None),
        P(),
        P("group", "sample", None),
        P("group"),
        P(None, "group", "sample", None),
    )
    out_specs = P(None, "group", "sample", None)
    return jax.shard_map(shards, mesh=mesh, in_specs=in_specs, out_specs=out_specs, check_vma=False)
```

```python
import functools

import jax
import jax.numpy as jnp
import numpy as np
from jax import lax
from jax.experimental import pallas as pl
from jax.experimental.pallas import tpu as pltpu
from jax.sharding import PartitionSpec as P

D = 2880
HEAD = 64
QHEADS = 8
AXES = ("group", "sample")
TILE = 6480
IN_ROWS = 2880
IN_SIZE = 2880 * 640
SLOT = 56
USED = 55
ROWS = 32
VMEM = pl.BlockSpec(memory_space=pltpu.VMEM)
SMEM = pl.BlockSpec(memory_space=pltpu.SMEM)
MIB = 1024 * 1024


def device_id(z, y, x, core):
    return z * 32 + (y % 2) * 16 + (y // 2) * 8 + x * 2 + core


Z_GROUPS = [
    [device_id(z, y, x, c) for z in range(16)] for y in range(4) for x in range(4) for c in range(2)
]


def line_groups(x_core):
    along_x = [[device_id(z, y, x, x_core) for x in range(4)] for z in range(16) for y in range(4)]
    along_y = [
        [device_id(z, y, x, 1 - x_core) for y in range(4)] for z in range(16) for x in range(4)
    ]
    return along_x + along_y


def moves(step):
    pairs = []
    for z in range(16):
        for y in range(4):
            for x in range(4):
                for c in range(2):
                    y2, x2, c2 = step(y, x, c)
                    pairs.append((device_id(z, y, x, c), device_id(z, y2 % 4, x2 % 4, c2)))
    return pairs


CORE_SWAP = moves(lambda y, x, c: (y, x, 1 - c))
X_OUT = moves(lambda y, x, c: (y, x - 1 if c else x + 1, c))
X_BACK = moves(lambda y, x, c: (y, x + 1 if c else x - 1, c))
Y_FAR = moves(lambda y, x, c: (y + 2, x, c))
RING_UP = moves(lambda y, x, c: (y, x + 1, c) if c else (y + 1, x, c))
RING_DOWN = moves(lambda y, x, c: (y, x - 1, c) if c else (y - 1, x, c))


def form_kernel(matching_ref, tile_ref, out_ref, buf_ref):
    me = lax.axis_index("group") * 16 + lax.axis_index("sample")
    place = matching_ref[me]
    buf_ref[...] = jnp.zeros((64, 128), jnp.float32)
    for r in range(50):
        buf_ref[r : r + 1, :] = tile_ref[:, 128 * r : 128 * r + 128].astype(jnp.float32)
    buf_ref[50:51, :80] = tile_ref[:, 6400:6480].astype(jnp.float32)
    raw = buf_ref[...]
    row = lax.broadcasted_iota(jnp.int32, (64, 128), 0)
    lane = lax.broadcasted_iota(jnp.int32, (64, 128), 1)
    in_len = jnp.clip(IN_SIZE - TILE * place, 0, TILE)
    part = jnp.where(row * 128 + lane < in_len, raw, 0.0)
    shift = 80 * (place & 7)
    lanes = shift & 127
    turned = pltpu.roll(part, lanes, 1)
    above = pltpu.roll(turned, 1, 0)
    shifted = pltpu.roll(jnp.where(lane >= lanes, turned, above), shift >> 7, 0)
    units = []
    lane8 = lax.broadcasted_iota(jnp.int32, (8, 128), 1)
    row8 = lax.broadcasted_iota(jnp.int32, (8, 128), 0)
    for i in range(9):
        base, off = divmod(720 * i, 128)
        window = buf_ref[base : base + 8, :]
        if off:
            window = pltpu.roll(window, 128 - off, 1)
            below = pltpu.roll(window, 7, 0)
            window = jnp.where(lane8 < 128 - off, window, below)
        units.append(jnp.where((row8 < 5) | (lane8 < 80), window, 0.0)[:6])
    for i in range(9):
        buf_ref[1 + 6 * i : 7 + 6 * i, :] = units[i]
    first = 1 + 6 * jnp.clip(2560 - 9 * place, 0, 9)
    out = jnp.where((row >= first) & (row < 55), buf_ref[...], 0.0) + shifted
    out = out[:SLOT].astype(jnp.bfloat16)
    for j in range(out_ref.shape[0]):
        out_ref[j] = out


def merge_kernel(in_ref, out_ref, buf_ref):
    for j in range(16):
        buf_ref[SLOT * j : SLOT * j + SLOT, :] = in_ref[j].astype(jnp.float32)
    for r in range(USED):
        low = buf_ref[pl.ds(r, 8, stride=SLOT), :]
        high = buf_ref[pl.ds(r + 8 * SLOT, 8, stride=SLOT), :]
        both = jnp.concatenate([low, high], 0).astype(jnp.bfloat16)
        for k in range(out_ref.shape[0]):
            out_ref[k, r] = both


def read_weights(refs, rows):
    columns = []
    for r in rows:
        columns.append(jnp.concatenate([ref[:, r].reshape(-1, 128) for ref in refs], 0))
    return jnp.concatenate(columns, 1)


def chip_place():
    group, sample = lax.axis_index("group"), lax.axis_index("sample")
    core = sample & 1
    x = (sample >> 1) & 3
    y = (sample >> 3) * 2 + (group & 1)
    return y, x, core


def ring_offset(piece):
    return jnp.where(piece == 0, 0, jnp.where(piece == 1, 3, piece - 1))


def slot_places(matching_row):
    y0, x0, core0 = chip_place()
    slot = lax.broadcasted_iota(jnp.int32, (1, 512), 1)
    core = core0 ^ (slot >> 8)
    offset = ring_offset((slot >> 6) & 3)
    line = (slot >> 4) & 3
    y = jnp.where(core == 0, (y0 + offset) & 3, line)
    x = jnp.where(core == 0, line, (x0 + offset) & 3)
    device = (slot & 15) * 32 + (y & 1) * 16 + (y >> 1) * 8 + x * 2 + core
    rows = lax.broadcasted_iota(jnp.int32, (512, 512), 0)
    chosen = jnp.where(rows == device, 1.0, 0.0).astype(jnp.bfloat16)
    row = lax.broadcasted_iota(jnp.int32, (8, 512), 0)
    digits = jnp.where(row == 0, matching_row >> 4, jnp.where(row == 1, matching_row & 15, 0))
    picked = jnp.dot(
        digits.astype(jnp.float32).astype(jnp.bfloat16), chosen, preferred_element_type=jnp.float32
    ).astype(jnp.int32)
    return picked[0:1] * 16 + picked[1:2]


def pick_kernel(x_ref, matching_ref, xg_ref, place_ref, xs_ref, a_ref):
    place = slot_places(matching_ref[...])
    place_ref[...] = place
    xs_ref[:, 2816:] = jnp.zeros((ROWS, 256), jnp.float32)
    xs_ref[:, :D] = x_ref[...].astype(jnp.float32).reshape(ROWS, D)
    xs = xs_ref[...]
    for i in range(11):
        moved = xs if i == 0 else pltpu.roll(xs, 3072 - i, 1)
        a_ref[ROWS * i : ROWS * i + ROWS, :] = moved.astype(jnp.bfloat16)
    start = jnp.where(place <= 284, 10 * place + (place >> 3), -1)
    total = None
    for k in range(12):
        rows = lax.broadcasted_iota(jnp.int32, (256, 512), 0) + 256 * k
        chosen = jnp.where(rows == start, 1.0, 0.0).astype(jnp.bfloat16)
        term = jnp.dot(
            a_ref[:, 256 * k : 256 * k + 256], chosen, preferred_element_type=jnp.float32
        )
        total = term if total is None else total + term
    xg_ref[...] = total.astype(jnp.bfloat16)


def project(xg_ref, halves):
    blocks = []
    for cols in ((0, 1), (2, 3), (4,)):
        total = None
        for half in range(2):
            for i in range(11):
                term = jnp.dot(
                    xg_ref[ROWS * i : ROWS * i + ROWS, 256 * half : 256 * half + 256],
                    read_weights(halves[half], [5 * i + b for b in cols]),
                    preferred_element_type=jnp.float32,
                )
                total = term if total is None else total + term
        blocks.append(total)
    return jnp.concatenate(blocks, 1)


CHUNK = 1024
SHARD = 512


def tail_kernel(
    limit_ref, xg_ref, place_ref, m0, m1, m2, m3, o0, o1, o2, o3, near_ref, far_ref, out_ref,
    s_ref, w_ref, og_ref, acc_ref,
):
    halves = ((m0, m1, m2, m3), (o0, o1, o2, o3))
    projected = project(xg_ref, halves)
    y0, x0, core0 = chip_place()
    rounded = projected.astype(jnp.bfloat16)
    own_kv = rounded[:, 512:640]
    heads = []
    zero = jnp.zeros((ROWS, HEAD), jnp.float32)
    for h in range(QHEADS):
        heads.append(jnp.concatenate([projected[:, HEAD * h : HEAD * h + HEAD], zero], 1))
    query = jnp.concatenate(heads, 0).astype(jnp.bfloat16)
    count = QHEADS * ROWS
    scale = np.float32(HEAD**-0.5 * np.log2(np.e))
    contract = (((1,), (1,)), ((), ()))
    limit = limit_ref[0] * 128

    own = lax.dot_general(query, own_kv, contract, preferred_element_type=jnp.float32)
    row = lax.broadcasted_iota(jnp.int32, (count, ROWS), 0)
    col = lax.broadcasted_iota(jnp.int32, (count, ROWS), 1)
    allowed = ((row & 7) == (col & 7)) & ((col >> 3) <= ((row >> 3) & 3))
    own = jnp.where(allowed, own, -1e30)

    chunks = 16 * SHARD // CHUNK
    def read_keys(k):
        ref = near_ref if k < chunks // 2 else far_ref
        first = CHUNK * (k % (chunks // 2))
        return ref[first : first + CHUNK, :]

    peak = jnp.full((count, 128), -1e30, jnp.float32)
    for k in range(chunks):
        scores = lax.dot_general(
            query, read_keys(k), contract, preferred_element_type=jnp.float32
        )
        bias = []
        for n in range(CHUNK // SHARD * k, CHUNK // SHARD * (k + 1)):
            core = core0 ^ (n >> 3)
            offset = (0, 3 - 2 * core, 1 + 2 * core, 2)[(n >> 1) & 3]
            shard = ((y0 >> 1) ^ (n & 1)) * 8 + ((x0 + offset) & 3) * 2 + core
            keys = lax.broadcasted_iota(jnp.int32, (1, SHARD), 1)
            bias.append(jnp.where(keys < limit - SHARD * shard, 0.0, -1e30))
        scores = scores + jnp.concatenate(bias, 1)
        s_ref[:, CHUNK * k : CHUNK * k + CHUNK] = scores
        for n in range(CHUNK // 128):
            peak = jnp.maximum(peak, scores[:, 128 * n : 128 * n + 128])
    top = jnp.maximum(jnp.max(peak, 1, keepdims=True), jnp.max(own, 1, keepdims=True))
    floor = top * scale

    ones = jnp.float32(1)

    def with_ones(piece):
        lane = lax.broadcasted_iota(jnp.int32, piece.shape, 1)
        return jnp.where(lane < HEAD, ones, piece.astype(jnp.float32)).astype(jnp.bfloat16)

    weights = jnp.where(allowed, jnp.exp2(own * scale - floor), 0.0).astype(jnp.bfloat16)
    summed = jnp.dot(weights, with_ones(own_kv), preferred_element_type=jnp.float32)
    for k in range(chunks):
        weights = jnp.exp2(s_ref[:, CHUNK * k : CHUNK * k + CHUNK] * scale - floor)
        summed = summed + jnp.dot(
            weights.astype(jnp.bfloat16),
            with_ones(read_keys(k)),
            preferred_element_type=jnp.float32,
        )
    mixed = summed[:, HEAD:] / summed[:, :HEAD]
    og_ref[...] = jnp.zeros(og_ref.shape, jnp.float32)
    for h in range(QHEADS):
        og_ref[:, 128 + HEAD * h : 128 + HEAD * h + HEAD] = mixed[ROWS * h : ROWS * h + ROWS]

    place = place_ref[...]
    unit = 9 * place - 2560
    base = (unit >> 2) + 1
    shown = jnp.where(place >= 284, base, -1)
    padded = og_ref[...]
    moved = [
        pltpu.roll(padded, 1, 1)[:, 128:640],
        padded[:, 128:640],
        pltpu.roll(padded, 767, 1)[:, 128:640],
    ]
    stacked = jnp.concatenate(moved, 0).astype(jnp.bfloat16)
    chosen = jnp.where(
        lax.broadcasted_iota(jnp.int32, (512, 512), 0) == shown, 1.0, 0.0
    ).astype(jnp.bfloat16)
    picked = jnp.dot(stacked, chosen, preferred_element_type=jnp.float32)
    phase = unit & 3
    for i in range(9):
        for c in range(4):
            wanted = (c - i) % 4
            d = (wanted + i) // 4
            w_ref[ROWS * c : ROWS * c + ROWS, 512 * i : 512 * i + 512] = jnp.where(
                phase == wanted, picked[ROWS * d : ROWS * d + ROWS], 0.0
            ).astype(jnp.bfloat16)
    acc_ref[...] = jnp.zeros(acc_ref.shape, jnp.float32)
    sides = []
    for cols in ((0, 1), (2, 3), (4, 5)):
        total = None
        for i in range(9):
            for half in range(2):
                term = jnp.dot(
                    w_ref[:, 512 * i + 256 * half : 512 * i + 256 * half + 256],
                    read_weights(halves[half], [1 + 6 * i + b for b in cols]),
                    preferred_element_type=jnp.float32,
                )
                total = term if total is None else total + term
        sides.append(total)
    sides.append(jnp.zeros((4 * ROWS, 128), jnp.float32))
    wide = jnp.concatenate(sides, 1)
    for c in range(4):
        first, off = divmod(720 * c, 128)
        block = wide[ROWS * c : ROWS * c + ROWS]
        if off:
            block = pltpu.roll(block, off, 1)
        span = pl.ds(128 * first, 896)
        acc_ref[:, span] = acc_ref[:, span] + block
    out_ref[...] = acc_ref[:, :D].reshape(out_ref.shape).astype(jnp.bfloat16)


def shards(trainer_flat, matching, prefix_kv, prefix_blocks, inputs):
    bf16, f32 = jnp.bfloat16, jnp.float32
    core = lax.axis_index("sample") % 2
    by_place = matching.reshape(16, 2, 2, 4, 2)
    half0 = by_place[..., 0].transpose(2, 1, 3, 0).reshape(1, 256)
    half1 = by_place[..., 1].transpose(3, 2, 1, 0).reshape(1, 256)
    places = jnp.where(
        core == 0, jnp.concatenate([half0, half1], 1), jnp.concatenate([half1, half0], 1)
    )
    x = inputs[:, 0]
    x = inputs[:, 0]
    prefix = prefix_kv[0]
    pair = lax.concatenate([prefix, lax.ppermute(prefix, AXES, Y_FAR)], 0)
    behind = lax.ppermute(pair, AXES, X_OUT)
    ahead = lax.ppermute(pair, AXES, X_BACK)
    across = lax.ppermute(behind, AXES, X_OUT)
    core_keys = lax.concatenate([pair, behind, ahead, across], 0)

    formed = pl.pallas_call(
        form_kernel,
        out_shape=jax.ShapeDtypeStruct((16, SLOT, 128), bf16),
        in_specs=[SMEM, VMEM],
        out_specs=VMEM,
        scratch_shapes=[pltpu.VMEM((64, 128), f32)],
        name="form",
    )(matching, trainer_flat)
    along_z = lax.all_to_all(formed, AXES, 0, 0, tiled=True, axis_index_groups=Z_GROUPS)
    merged = pl.pallas_call(
        merge_kernel,
        out_shape=jax.ShapeDtypeStruct((4, USED, 16, 128), bf16),
        in_specs=[VMEM],
        out_specs=VMEM,
        scratch_shapes=[pltpu.VMEM((16 * SLOT, 128), f32)],
        compiler_params=pltpu.CompilerParams(vmem_limit_bytes=8 * MIB),
        name="merge",
    )(along_z)
    lines = lax.all_to_all(merged, AXES, 0, 0, tiled=True, axis_index_groups=line_groups(0))
    lines, core_keys = lax.optimization_barrier((lines, core_keys))
    low = lax.ppermute(lines, AXES, RING_UP)
    high = lax.ppermute(lines, AXES, RING_DOWN)
    other_lines = lax.ppermute(lines, AXES, CORE_SWAP)
    other_keys = lax.ppermute(core_keys, AXES, CORE_SWAP)
    gathered, places = pl.pallas_call(
        pick_kernel,
        out_shape=(
            jax.ShapeDtypeStruct((11 * ROWS, 512), bf16),
            jax.ShapeDtypeStruct((1, 512), jnp.int32),
        ),
        in_specs=[VMEM] * 2,
        out_specs=(VMEM, VMEM),
        scratch_shapes=[pltpu.VMEM((ROWS, 3072), f32), pltpu.VMEM((11 * ROWS, 3072), bf16)],
        compiler_params=pltpu.CompilerParams(vmem_limit_bytes=12 * MIB),
        name="pick",
    )(x, matching.reshape(1, 512))
    low, gathered = lax.optimization_barrier((low, gathered))
    end0 = lax.ppermute(low[:2], AXES, RING_UP)
    end1 = lax.ppermute(high[2:], AXES, RING_DOWN)
    side, other_keys, other_lines = lax.optimization_barrier((low, other_keys, other_lines))
    other_low = lax.ppermute(side, AXES, CORE_SWAP)
    other_high = lax.ppermute(high, AXES, CORE_SWAP)
    ends = lax.concatenate([end0, end1], 0)
    other_ends = lax.ppermute(ends, AXES, CORE_SWAP)
    mine = [lines, low, high, ends]
    other = [other_lines, other_low, other_high, other_ends]
    output = pl.pallas_call(
        tail_kernel,
        out_shape=jax.ShapeDtypeStruct(x.shape, bf16),
        in_specs=[SMEM] + [VMEM] * 12,
        out_specs=VMEM,
        scratch_shapes=[
            pltpu.VMEM((QHEADS * ROWS, 16 * SHARD), f32),
            pltpu.VMEM((4 * ROWS, 9 * 512), bf16),
            pltpu.VMEM((ROWS, 768), f32),
            pltpu.VMEM((ROWS, 3072), f32),
        ],
        compiler_params=pltpu.CompilerParams(vmem_limit_bytes=20 * MIB),
        name="tail",
    )(prefix_blocks, gathered, places, *mine, *other, core_keys, other_keys)
    return output[:, None]


def solution(mesh):
    in_specs = (
        P(("group", "sample"), None),
        P(),
        P("group", "sample", None),
        P("group"),
        P(None, "group", "sample", None),
    )
    out_specs = P(None, "group", "sample", None)
    return jax.shard_map(shards, mesh=mesh, in_specs=in_specs, out_specs=out_specs, check_vma=False)
```

```python
import functools

import jax
import jax.numpy as jnp
import numpy as np
from jax import lax
from jax.experimental import pallas as pl
from jax.experimental.pallas import tpu as pltpu
from jax.sharding import PartitionSpec as P

D = 2880
HEAD = 64
QHEADS = 8
AXES = ("group", "sample")
TILE = 6480
IN_ROWS = 2880
IN_SIZE = 2880 * 640
SLOT = 56
USED = 55
ROWS = 32
VMEM = pl.BlockSpec(memory_space=pltpu.VMEM)
SMEM = pl.BlockSpec(memory_space=pltpu.SMEM)
MIB = 1024 * 1024


def device_id(z, y, x, core):
    return z * 32 + (y % 2) * 16 + (y // 2) * 8 + x * 2 + core


Z_GROUPS = [
    [device_id(z, y, x, c) for z in range(16)] for y in range(4) for x in range(4) for c in range(2)
]


def line_groups(x_core):
    along_x = [[device_id(z, y, x, x_core) for x in range(4)] for z in range(16) for y in range(4)]
    along_y = [
        [device_id(z, y, x, 1 - x_core) for y in range(4)] for z in range(16) for x in range(4)
    ]
    return along_x + along_y


def moves(step):
    pairs = []
    for z in range(16):
        for y in range(4):
            for x in range(4):
                for c in range(2):
                    y2, x2, c2 = step(y, x, c)
                    pairs.append((device_id(z, y, x, c), device_id(z, y2 % 4, x2 % 4, c2)))
    return pairs


CORE_SWAP = moves(lambda y, x, c: (y, x, 1 - c))
X_OUT = moves(lambda y, x, c: (y, x - 1 if c else x + 1, c))
X_BACK = moves(lambda y, x, c: (y, x + 1 if c else x - 1, c))
Y_FAR = moves(lambda y, x, c: (y + 2, x, c))
RING_UP = moves(lambda y, x, c: (y, x + 1, c) if c else (y + 1, x, c))
RING_FAR = moves(lambda y, x, c: (y, x + 2, c) if c else (y + 2, x, c))
RING_DOWN = moves(lambda y, x, c: (y, x - 1, c) if c else (y - 1, x, c))


def form_kernel(matching_ref, tile_ref, out_ref, buf_ref):
    me = lax.axis_index("group") * 16 + lax.axis_index("sample")
    place = matching_ref[me]
    buf_ref[...] = jnp.zeros((64, 128), jnp.float32)
    for r in range(50):
        buf_ref[r : r + 1, :] = tile_ref[:, 128 * r : 128 * r + 128].astype(jnp.float32)
    buf_ref[50:51, :80] = tile_ref[:, 6400:6480].astype(jnp.float32)
    raw = buf_ref[...]
    row = lax.broadcasted_iota(jnp.int32, (64, 128), 0)
    lane = lax.broadcasted_iota(jnp.int32, (64, 128), 1)
    in_len = jnp.clip(IN_SIZE - TILE * place, 0, TILE)
    part = jnp.where(row * 128 + lane < in_len, raw, 0.0)
    shift = 80 * (place & 7)
    lanes = shift & 127
    turned = pltpu.roll(part, lanes, 1)
    above = pltpu.roll(turned, 1, 0)
    shifted = pltpu.roll(jnp.where(lane >= lanes, turned, above), shift >> 7, 0)
    units = []
    lane8 = lax.broadcasted_iota(jnp.int32, (8, 128), 1)
    row8 = lax.broadcasted_iota(jnp.int32, (8, 128), 0)
    for i in range(9):
        base, off = divmod(720 * i, 128)
        window = buf_ref[base : base + 8, :]
        if off:
            window = pltpu.roll(window, 128 - off, 1)
            below = pltpu.roll(window, 7, 0)
            window = jnp.where(lane8 < 128 - off, window, below)
        units.append(jnp.where((row8 < 5) | (lane8 < 80), window, 0.0)[:6])
    for i in range(9):
        buf_ref[1 + 6 * i : 7 + 6 * i, :] = units[i]
    first = 1 + 6 * jnp.clip(2560 - 9 * place, 0, 9)
    out = jnp.where((row >= first) & (row < 55), buf_ref[...], 0.0) + shifted
    out = out[:SLOT].astype(jnp.bfloat16)
    for j in range(out_ref.shape[0]):
        out_ref[j] = out


def merge_kernel(in_ref, out_ref, buf_ref):
    for j in range(16):
        buf_ref[SLOT * j : SLOT * j + SLOT, :] = in_ref[j].astype(jnp.float32)
    for r in range(USED):
        low = buf_ref[pl.ds(r, 8, stride=SLOT), :]
        high = buf_ref[pl.ds(r + 8 * SLOT, 8, stride=SLOT), :]
        both = jnp.concatenate([low, high], 0).astype(jnp.bfloat16)
        for k in range(out_ref.shape[0]):
            out_ref[k, r] = both


def read_weights(refs, rows):
    columns = []
    for r in rows:
        columns.append(jnp.concatenate([ref[:, r].reshape(-1, 128) for ref in refs], 0))
    return jnp.concatenate(columns, 1)


def chip_place():
    group, sample = lax.axis_index("group"), lax.axis_index("sample")
    core = sample & 1
    x = (sample >> 1) & 3
    y = (sample >> 3) * 2 + (group & 1)
    return y, x, core


def ring_offset(piece):
    return jnp.where(piece == 0, 0, jnp.where(piece == 1, 3, piece - 1))


def slot_places(matching_row):
    y0, x0, core0 = chip_place()
    slot = lax.broadcasted_iota(jnp.int32, (1, 512), 1)
    core = core0 ^ (slot >> 8)
    offset = ring_offset((slot >> 6) & 3)
    line = (slot >> 4) & 3
    y = jnp.where(core == 0, (y0 + offset) & 3, line)
    x = jnp.where(core == 0, line, (x0 + offset) & 3)
    device = (slot & 15) * 32 + (y & 1) * 16 + (y >> 1) * 8 + x * 2 + core
    rows = lax.broadcasted_iota(jnp.int32, (512, 512), 0)
    chosen = jnp.where(rows == device, 1.0, 0.0).astype(jnp.bfloat16)
    row = lax.broadcasted_iota(jnp.int32, (8, 512), 0)
    digits = jnp.where(row == 0, matching_row >> 4, jnp.where(row == 1, matching_row & 15, 0))
    picked = jnp.dot(
        digits.astype(jnp.float32).astype(jnp.bfloat16), chosen, preferred_element_type=jnp.float32
    ).astype(jnp.int32)
    return picked[0:1] * 16 + picked[1:2]


def pick_kernel(x_ref, matching_ref, xg_ref, place_ref, row_ref, xs_ref, a_ref):
    place = slot_places(matching_ref[...])
    place_ref[...] = place
    row = jnp.where(place >= 284, ((9 * place - 2560) >> 2) + 1, -1)
    row_ref[...] = jnp.where(
        lax.broadcasted_iota(jnp.int32, (512, 512), 0) == row, 1.0, 0.0
    ).astype(jnp.bfloat16)
    xs_ref[:, 2816:] = jnp.zeros((ROWS, 256), jnp.float32)
    xs_ref[:, :D] = x_ref[...].astype(jnp.float32).reshape(ROWS, D)
    xs = xs_ref[...]
    for i in range(11):
        moved = xs if i == 0 else pltpu.roll(xs, 3072 - i, 1)
        a_ref[ROWS * i : ROWS * i + ROWS, :] = moved.astype(jnp.bfloat16)
    start = jnp.where(place <= 284, 10 * place + (place >> 3), -1)
    total = None
    for k in range(12):
        rows = lax.broadcasted_iota(jnp.int32, (256, 512), 0) + 256 * k
        chosen = jnp.where(rows == start, 1.0, 0.0).astype(jnp.bfloat16)
        term = jnp.dot(
            a_ref[:, 256 * k : 256 * k + 256], chosen, preferred_element_type=jnp.float32
        )
        total = term if total is None else total + term
    xg_ref[...] = total.astype(jnp.bfloat16)


def project(xg_ref, halves):
    blocks = []
    for cols in ((0, 1), (2, 3), (4,)):
        total = None
        for half in range(2):
            for i in range(11):
                term = jnp.dot(
                    xg_ref[ROWS * i : ROWS * i + ROWS, 256 * half : 256 * half + 256],
                    read_weights(halves[half], [5 * i + b for b in cols]),
                    preferred_element_type=jnp.float32,
                )
                total = term if total is None else total + term
        blocks.append(total)
    return jnp.concatenate(blocks, 1)


CHUNK = 1024
SHARD = 512


def tail_kernel(
    limit_ref, xg_ref, place_ref, row_ref, m0, m1, m2, m3, o0, o1, o2, o3, near_ref, far_ref, out_ref,
    s_ref, w_ref, og_ref, acc_ref,
):
    halves = ((m0, m1, m2, m3), (o0, o1, o2, o3))
    projected = project(xg_ref, halves)
    y0, x0, core0 = chip_place()
    rounded = projected.astype(jnp.bfloat16)
    own_kv = rounded[:, 512:640]
    heads = []
    zero = jnp.zeros((ROWS, HEAD), jnp.float32)
    for h in range(QHEADS):
        heads.append(jnp.concatenate([projected[:, HEAD * h : HEAD * h + HEAD], zero], 1))
    query = jnp.concatenate(heads, 0).astype(jnp.bfloat16)
    count = QHEADS * ROWS
    scale = np.float32(HEAD**-0.5 * np.log2(np.e))
    contract = (((1,), (1,)), ((), ()))
    limit = limit_ref[0] * 128

    own = lax.dot_general(query, own_kv, contract, preferred_element_type=jnp.float32)
    row = lax.broadcasted_iota(jnp.int32, (count, ROWS), 0)
    col = lax.broadcasted_iota(jnp.int32, (count, ROWS), 1)
    allowed = ((row & 7) == (col & 7)) & ((col >> 3) <= ((row >> 3) & 3))
    own = jnp.where(allowed, own, -1e30)

    chunks = 16 * SHARD // CHUNK
    def read_keys(k):
        ref = near_ref if k < chunks // 2 else far_ref
        first = CHUNK * (k % (chunks // 2))
        return ref[first : first + CHUNK, :]

    peak = jnp.full((count, 128), -1e30, jnp.float32)
    for k in range(chunks):
        scores = lax.dot_general(
            query, read_keys(k), contract, preferred_element_type=jnp.float32
        )
        bias = []
        for n in range(CHUNK // SHARD * k, CHUNK // SHARD * (k + 1)):
            core = core0 ^ (n >> 3)
            offset = (0, 3 - 2 * core, 1 + 2 * core, 2)[(n >> 1) & 3]
            shard = ((y0 >> 1) ^ (n & 1)) * 8 + ((x0 + offset) & 3) * 2 + core
            keys = lax.broadcasted_iota(jnp.int32, (1, SHARD), 1)
            bias.append(jnp.where(keys < limit - SHARD * shard, 0.0, -1e30))
        scores = scores + jnp.concatenate(bias, 1)
        s_ref[:, CHUNK * k : CHUNK * k + CHUNK] = scores
        for n in range(CHUNK // 128):
            peak = jnp.maximum(peak, scores[:, 128 * n : 128 * n + 128])
    top = jnp.maximum(jnp.max(peak, 1, keepdims=True), jnp.max(own, 1, keepdims=True))
    floor = top * scale

    lane = lax.broadcasted_iota(jnp.int32, (1, 128), 1)
    kept = jnp.where(lane < HEAD, 0.0, 1.0).astype(jnp.bfloat16)
    ones = jnp.where(lane < HEAD, 1.0, 0.0).astype(jnp.bfloat16)

    def with_ones(piece):
        return piece * kept + ones

    weights = jnp.where(allowed, jnp.exp2(own * scale - floor), 0.0).astype(jnp.bfloat16)
    summed = jnp.dot(weights, with_ones(own_kv), preferred_element_type=jnp.float32)
    for k in range(chunks):
        powers = s_ref[:, CHUNK * k : CHUNK * k + CHUNK] * scale - floor
        weights = jnp.exp2(powers.astype(jnp.bfloat16))
        summed = summed + jnp.dot(
            weights,
            with_ones(read_keys(k)),
            preferred_element_type=jnp.float32,
        )
    mixed = summed[:, HEAD:] / summed[:, :HEAD]
    og_ref[...] = jnp.zeros(og_ref.shape, jnp.float32)
    for h in range(QHEADS):
        og_ref[:, 128 + HEAD * h : 128 + HEAD * h + HEAD] = mixed[ROWS * h : ROWS * h + ROWS]

    place = place_ref[...]
    unit = 9 * place - 2560
    padded = og_ref[...]
    moved = [
        pltpu.roll(padded, 1, 1)[:, 128:640],
        padded[:, 128:640],
        pltpu.roll(padded, 767, 1)[:, 128:640],
    ]
    stacked = jnp.concatenate(moved, 0).astype(jnp.bfloat16)
    picked = jnp.dot(stacked, row_ref[...], preferred_element_type=jnp.float32)
    phase = unit & 3
    for i in range(9):
        for c in range(4):
            wanted = (c - i) % 4
            d = (wanted + i) // 4
            w_ref[ROWS * c : ROWS * c + ROWS, 512 * i : 512 * i + 512] = jnp.where(
                phase == wanted, picked[ROWS * d : ROWS * d + ROWS], 0.0
            ).astype(jnp.bfloat16)
    acc_ref[...] = jnp.zeros(acc_ref.shape, jnp.float32)
    sides = []
    for cols in ((0, 1), (2, 3), (4, 5)):
        total = None
        for i in range(9):
            for half in range(2):
                term = jnp.dot(
                    w_ref[:, 512 * i + 256 * half : 512 * i + 256 * half + 256],
                    read_weights(halves[half], [1 + 6 * i + b for b in cols]),
                    preferred_element_type=jnp.float32,
                )
                total = term if total is None else total + term
        sides.append(total)
    sides.append(jnp.zeros((4 * ROWS, 128), jnp.float32))
    wide = jnp.concatenate(sides, 1)
    for c in range(4):
        first, off = divmod(720 * c, 128)
        block = wide[ROWS * c : ROWS * c + ROWS]
        if off:
            block = pltpu.roll(block, off, 1)
        span = pl.ds(128 * first, 896)
        acc_ref[:, span] = acc_ref[:, span] + block
    out_ref[...] = acc_ref[:, :D].reshape(out_ref.shape).astype(jnp.bfloat16)


def shards(trainer_flat, matching, prefix_kv, prefix_blocks, inputs):
    bf16, f32 = jnp.bfloat16, jnp.float32
    core = lax.axis_index("sample") % 2
    by_place = matching.reshape(16, 2, 2, 4, 2)
    half0 = by_place[..., 0].transpose(2, 1, 3, 0).reshape(1, 256)
    half1 = by_place[..., 1].transpose(3, 2, 1, 0).reshape(1, 256)
    places = jnp.where(
        core == 0, jnp.concatenate([half0, half1], 1), jnp.concatenate([half1, half0], 1)
    )
    x = inputs[:, 0]
    prefix = prefix_kv[0]
    pair = lax.concatenate([prefix, lax.ppermute(prefix, AXES, Y_FAR)], 0)
    behind = lax.ppermute(pair, AXES, X_OUT)
    ahead = lax.ppermute(pair, AXES, X_BACK)
    across = lax.ppermute(behind, AXES, X_OUT)
    core_keys = lax.concatenate([pair, behind, ahead, across], 0)

    formed = pl.pallas_call(
        form_kernel,
        out_shape=jax.ShapeDtypeStruct((16, SLOT, 128), bf16),
        in_specs=[SMEM, VMEM],
        out_specs=VMEM,
        scratch_shapes=[pltpu.VMEM((64, 128), f32)],
        name="form",
    )(matching, trainer_flat)
    along_z = lax.all_to_all(formed, AXES, 0, 0, tiled=True, axis_index_groups=Z_GROUPS)
    merged = pl.pallas_call(
        merge_kernel,
        out_shape=jax.ShapeDtypeStruct((4, USED, 16, 128), bf16),
        in_specs=[VMEM],
        out_specs=VMEM,
        scratch_shapes=[pltpu.VMEM((16 * SLOT, 128), f32)],
        compiler_params=pltpu.CompilerParams(vmem_limit_bytes=8 * MIB),
        name="merge",
    )(along_z)
    lines = lax.all_to_all(merged, AXES, 0, 0, tiled=True, axis_index_groups=line_groups(0))
    lines, core_keys = lax.optimization_barrier((lines, core_keys))
    low = lax.ppermute(lines, AXES, RING_UP)
    high = lax.ppermute(lines, AXES, RING_DOWN)
    end1 = lax.ppermute(lines[2:], AXES, RING_FAR)
    x, _ = lax.optimization_barrier((inputs[:, 0], lines))
    gathered, places, out_rows = pl.pallas_call(
        pick_kernel,
        out_shape=(
            jax.ShapeDtypeStruct((11 * ROWS, 512), bf16),
            jax.ShapeDtypeStruct((1, 512), jnp.int32),
            jax.ShapeDtypeStruct((512, 512), bf16),
        ),
        in_specs=[VMEM] * 2,
        out_specs=(VMEM, VMEM, VMEM),
        scratch_shapes=[pltpu.VMEM((ROWS, 3072), f32), pltpu.VMEM((11 * ROWS, 3072), bf16)],
        compiler_params=pltpu.CompilerParams(vmem_limit_bytes=12 * MIB),
        name="pick",
    )(x, matching.reshape(1, 512))
    swapped, core_keys, _ = lax.optimization_barrier((lines, core_keys, gathered))
    other_lines = lax.ppermute(swapped, AXES, CORE_SWAP)
    other_keys = lax.ppermute(core_keys, AXES, CORE_SWAP)
    low, gathered = lax.optimization_barrier((low, gathered))
    end0 = lax.ppermute(low[:2], AXES, RING_UP)
    low, end1 = lax.optimization_barrier((low, end1))
    other_low = lax.ppermute(low, AXES, CORE_SWAP)
    other_high = lax.ppermute(high, AXES, CORE_SWAP)
    ends = lax.concatenate([end0, end1], 0)
    other_ends = lax.ppermute(ends, AXES, CORE_SWAP)
    mine = [lines, low, high, ends]
    other = [other_lines, other_low, other_high, other_ends]
    output = pl.pallas_call(
        tail_kernel,
        out_shape=jax.ShapeDtypeStruct(x.shape, bf16),
        in_specs=[SMEM] + [VMEM] * 13,
        out_specs=VMEM,
        scratch_shapes=[
            pltpu.VMEM((QHEADS * ROWS, 16 * SHARD), f32),
            pltpu.VMEM((4 * ROWS, 9 * 512), bf16),
            pltpu.VMEM((ROWS, 768), f32),
            pltpu.VMEM((ROWS, 3072), f32),
        ],
        compiler_params=pltpu.CompilerParams(vmem_limit_bytes=20 * MIB),
        name="tail",
    )(prefix_blocks, gathered, places, out_rows, *mine, *other, core_keys, other_keys)
    return output[:, None]


def solution(mesh):
    in_specs = (
        P(("group", "sample"), None),
        P(),
        P("group", "sample", None),
        P("group"),
        P(None, "group", "sample", None),
    )
    out_specs = P(None, "group", "sample", None)
    return jax.shard_map(shards, mesh=mesh, in_specs=in_specs, out_specs=out_specs, check_vma=False)
```

```python
import functools

import jax
import jax.numpy as jnp
import numpy as np
from jax import lax
from jax.experimental import pallas as pl
from jax.experimental.pallas import tpu as pltpu
from jax.sharding import PartitionSpec as P

D = 2880
HEAD = 64
QHEADS = 8
AXES = ("group", "sample")
TILE = 6480
IN_ROWS = 2880
IN_SIZE = 2880 * 640
SLOT = 56
USED = 55
ROWS = 32
VMEM = pl.BlockSpec(memory_space=pltpu.VMEM)
SMEM = pl.BlockSpec(memory_space=pltpu.SMEM)
MIB = 1024 * 1024


def device_id(z, y, x, core):
    return z * 32 + (y % 2) * 16 + (y // 2) * 8 + x * 2 + core


Z_GROUPS = [
    [device_id(z, y, x, c) for z in range(16)] for y in range(4) for x in range(4) for c in range(2)
]


def line_groups(x_core):
    along_x = [[device_id(z, y, x, x_core) for x in range(4)] for z in range(16) for y in range(4)]
    along_y = [
        [device_id(z, y, x, 1 - x_core) for y in range(4)] for z in range(16) for x in range(4)
    ]
    return along_x + along_y


def moves(step):
    pairs = []
    for z in range(16):
        for y in range(4):
            for x in range(4):
                for c in range(2):
                    y2, x2, c2 = step(y, x, c)
                    pairs.append((device_id(z, y, x, c), device_id(z, y2 % 4, x2 % 4, c2)))
    return pairs


CORE_SWAP = moves(lambda y, x, c: (y, x, 1 - c))
X_OUT = moves(lambda y, x, c: (y, x - 1 if c else x + 1, c))
X_BACK = moves(lambda y, x, c: (y, x + 1 if c else x - 1, c))
Y_FAR = moves(lambda y, x, c: (y + 2, x, c))
RING_UP = moves(lambda y, x, c: (y, x + 1, c) if c else (y + 1, x, c))
RING_FAR = moves(lambda y, x, c: (y, x + 2, c) if c else (y + 2, x, c))
RING_DOWN = moves(lambda y, x, c: (y, x - 1, c) if c else (y - 1, x, c))


def form_kernel(matching_ref, tile_ref, out_ref, buf_ref):
    me = lax.axis_index("group") * 16 + lax.axis_index("sample")
    place = matching_ref[me]
    buf_ref[...] = jnp.zeros((64, 128), jnp.float32)
    for r in range(50):
        buf_ref[r : r + 1, :] = tile_ref[:, 128 * r : 128 * r + 128].astype(jnp.float32)
    buf_ref[50:51, :80] = tile_ref[:, 6400:6480].astype(jnp.float32)
    raw = buf_ref[...]
    row = lax.broadcasted_iota(jnp.int32, (64, 128), 0)
    lane = lax.broadcasted_iota(jnp.int32, (64, 128), 1)
    in_len = jnp.clip(IN_SIZE - TILE * place, 0, TILE)
    part = jnp.where(row * 128 + lane < in_len, raw, 0.0)
    shift = 80 * (place & 7)
    lanes = shift & 127
    turned = pltpu.roll(part, lanes, 1)
    above = pltpu.roll(turned, 1, 0)
    shifted = pltpu.roll(jnp.where(lane >= lanes, turned, above), shift >> 7, 0)
    units = []
    lane8 = lax.broadcasted_iota(jnp.int32, (8, 128), 1)
    row8 = lax.broadcasted_iota(jnp.int32, (8, 128), 0)
    for i in range(9):
        base, off = divmod(720 * i, 128)
        window = buf_ref[base : base + 8, :]
        if off:
            window = pltpu.roll(window, 128 - off, 1)
            below = pltpu.roll(window, 7, 0)
            window = jnp.where(lane8 < 128 - off, window, below)
        units.append(jnp.where((row8 < 5) | (lane8 < 80), window, 0.0)[:6])
    for i in range(9):
        buf_ref[1 + 6 * i : 7 + 6 * i, :] = units[i]
    first = 1 + 6 * jnp.clip(2560 - 9 * place, 0, 9)
    out = jnp.where((row >= first) & (row < 55), buf_ref[...], 0.0) + shifted
    out = out[:SLOT].astype(jnp.bfloat16)
    for j in range(out_ref.shape[0]):
        out_ref[j] = out


def merge_kernel(in_ref, out_ref, buf_ref):
    for j in range(16):
        buf_ref[SLOT * j : SLOT * j + SLOT, :] = in_ref[j].astype(jnp.float32)
    for r in range(USED):
        low = buf_ref[pl.ds(r, 8, stride=SLOT), :]
        high = buf_ref[pl.ds(r + 8 * SLOT, 8, stride=SLOT), :]
        both = jnp.concatenate([low, high], 0).astype(jnp.bfloat16)
        for k in range(out_ref.shape[0]):
            out_ref[k, r] = both


def read_weights(refs, rows):
    columns = []
    for r in rows:
        columns.append(jnp.concatenate([ref[:, r].reshape(-1, 128) for ref in refs], 0))
    return jnp.concatenate(columns, 1)


def chip_place():
    group, sample = lax.axis_index("group"), lax.axis_index("sample")
    core = sample & 1
    x = (sample >> 1) & 3
    y = (sample >> 3) * 2 + (group & 1)
    return y, x, core


def ring_offset(piece):
    return jnp.where(piece == 0, 0, jnp.where(piece == 1, 3, piece - 1))


def slot_places(matching_row):
    y0, x0, core0 = chip_place()
    slot = lax.broadcasted_iota(jnp.int32, (1, 512), 1)
    core = core0 ^ (slot >> 8)
    offset = ring_offset((slot >> 6) & 3)
    line = (slot >> 4) & 3
    y = jnp.where(core == 0, (y0 + offset) & 3, line)
    x = jnp.where(core == 0, line, (x0 + offset) & 3)
    device = (slot & 15) * 32 + (y & 1) * 16 + (y >> 1) * 8 + x * 2 + core
    rows = lax.broadcasted_iota(jnp.int32, (512, 512), 0)
    chosen = jnp.where(rows == device, 1.0, 0.0).astype(jnp.bfloat16)
    row = lax.broadcasted_iota(jnp.int32, (8, 512), 0)
    digits = jnp.where(row == 0, matching_row >> 4, jnp.where(row == 1, matching_row & 15, 0))
    picked = jnp.dot(
        digits.astype(jnp.float32).astype(jnp.bfloat16), chosen, preferred_element_type=jnp.float32
    ).astype(jnp.int32)
    return picked[0:1] * 16 + picked[1:2]


def pick_kernel(x_ref, matching_ref, xg_ref, place_ref, row_ref, xs_ref, a_ref):
    place = slot_places(matching_ref[...])
    place_ref[...] = place
    row = jnp.where(place >= 284, ((9 * place - 2560) >> 2) + 1, -1)
    row_ref[...] = jnp.where(
        lax.broadcasted_iota(jnp.int32, (512, 512), 0) == row, 1.0, 0.0
    ).astype(jnp.bfloat16)
    xs_ref[:, 2816:] = jnp.zeros((ROWS, 256), jnp.float32)
    xs_ref[:, :D] = x_ref[...].astype(jnp.float32).reshape(ROWS, D)
    xs = xs_ref[...]
    for i in range(11):
        moved = xs if i == 0 else pltpu.roll(xs, 3072 - i, 1)
        a_ref[ROWS * i : ROWS * i + ROWS, :] = moved.astype(jnp.bfloat16)
    start = jnp.where(place <= 284, 10 * place + (place >> 3), -1)
    total = None
    for k in range(12):
        rows = lax.broadcasted_iota(jnp.int32, (256, 512), 0) + 256 * k
        chosen = jnp.where(rows == start, 1.0, 0.0).astype(jnp.bfloat16)
        term = jnp.dot(
            a_ref[:, 256 * k : 256 * k + 256], chosen, preferred_element_type=jnp.float32
        )
        total = term if total is None else total + term
    xg_ref[...] = total.astype(jnp.bfloat16)


def project(xg_ref, halves):
    blocks = []
    for cols in ((0, 1), (2, 3), (4,)):
        total = None
        for half in range(2):
            for i in range(11):
                term = jnp.dot(
                    xg_ref[ROWS * i : ROWS * i + ROWS, 256 * half : 256 * half + 256],
                    read_weights(halves[half], [5 * i + b for b in cols]),
                    preferred_element_type=jnp.float32,
                )
                total = term if total is None else total + term
        blocks.append(total)
    return jnp.concatenate(blocks, 1)


CHUNK = 1024
SHARD = 512


def tail_kernel(
    limit_ref, xg_ref, place_ref, row_ref, m0, m1, m2, m3, o0, o1, o2, o3, near_ref, far_ref, out_ref,
    s_ref, w_ref, og_ref, acc_ref,
):
    halves = ((m0, m1, m2, m3), (o0, o1, o2, o3))
    projected = project(xg_ref, halves)
    y0, x0, core0 = chip_place()
    rounded = projected.astype(jnp.bfloat16)
    own_kv = rounded[:, 512:640]
    heads = []
    zero = jnp.zeros((ROWS, HEAD), jnp.float32)
    for h in range(QHEADS):
        heads.append(jnp.concatenate([projected[:, HEAD * h : HEAD * h + HEAD], zero], 1))
    query = jnp.concatenate(heads, 0).astype(jnp.bfloat16)
    count = QHEADS * ROWS
    scale = np.float32(HEAD**-0.5 * np.log2(np.e))
    contract = (((1,), (1,)), ((), ()))
    limit = limit_ref[0] * 128

    own = lax.dot_general(query, own_kv, contract, preferred_element_type=jnp.float32)
    row = lax.broadcasted_iota(jnp.int32, (count, ROWS), 0)
    col = lax.broadcasted_iota(jnp.int32, (count, ROWS), 1)
    allowed = ((row & 7) == (col & 7)) & ((col >> 3) <= ((row >> 3) & 3))
    own = jnp.where(allowed, own, -1e30)

    chunks = 16 * SHARD // CHUNK
    def read_keys(k):
        ref = near_ref if k < chunks // 2 else far_ref
        first = CHUNK * (k % (chunks // 2))
        return ref[first : first + CHUNK, :]

    peak = jnp.full((count, 128), -1e30, jnp.float32)
    for k in range(chunks):
        scores = lax.dot_general(
            query, read_keys(k), contract, preferred_element_type=jnp.float32
        )
        bias = []
        for n in range(CHUNK // SHARD * k, CHUNK // SHARD * (k + 1)):
            core = core0 ^ (n >> 3)
            offset = (0, 3 - 2 * core, 1 + 2 * core, 2)[(n >> 1) & 3]
            shard = ((y0 >> 1) ^ (n & 1)) * 8 + ((x0 + offset) & 3) * 2 + core
            keys = lax.broadcasted_iota(jnp.int32, (1, SHARD), 1)
            bias.append(jnp.where(keys < limit - SHARD * shard, 0.0, -1e30))
        scores = scores + jnp.concatenate(bias, 1)
        s_ref[:, CHUNK * k : CHUNK * k + CHUNK] = scores
        for n in range(CHUNK // 128):
            peak = jnp.maximum(peak, scores[:, 128 * n : 128 * n + 128])
    top = jnp.maximum(jnp.max(peak, 1, keepdims=True), jnp.max(own, 1, keepdims=True))
    floor = top * scale

    lane = lax.broadcasted_iota(jnp.int32, (1, 128), 1)
    kept = jnp.where(lane < HEAD, 0.0, 1.0).astype(jnp.bfloat16)
    ones = jnp.where(lane < HEAD, 1.0, 0.0).astype(jnp.bfloat16)

    def with_ones(piece):
        return piece * kept + ones

    weights = jnp.where(allowed, jnp.exp2(own * scale - floor), 0.0).astype(jnp.bfloat16)
    summed = jnp.dot(weights, with_ones(own_kv), preferred_element_type=jnp.float32)
    for k in range(chunks):
        powers = s_ref[:, CHUNK * k : CHUNK * k + CHUNK] * scale - floor
        weights = jnp.exp2(powers.astype(jnp.bfloat16))
        summed = summed + jnp.dot(
            weights,
            with_ones(read_keys(k)),
            preferred_element_type=jnp.float32,
        )
    mixed = summed[:, HEAD:] / summed[:, :HEAD]
    og_ref[...] = jnp.zeros(og_ref.shape, jnp.float32)
    for h in range(QHEADS):
        og_ref[:, 128 + HEAD * h : 128 + HEAD * h + HEAD] = mixed[ROWS * h : ROWS * h + ROWS]

    place = place_ref[...]
    unit = 9 * place - 2560
    padded = og_ref[...]
    moved = [
        pltpu.roll(padded, 1, 1)[:, 128:640],
        padded[:, 128:640],
        pltpu.roll(padded, 767, 1)[:, 128:640],
    ]
    stacked = jnp.concatenate(moved, 0).astype(jnp.bfloat16)
    picked = jnp.dot(stacked, row_ref[...], preferred_element_type=jnp.float32)
    phase = unit & 3
    for i in range(9):
        for c in range(4):
            wanted = (c - i) % 4
            d = (wanted + i) // 4
            w_ref[ROWS * c : ROWS * c + ROWS, 512 * i : 512 * i + 512] = jnp.where(
                phase == wanted, picked[ROWS * d : ROWS * d + ROWS], 0.0
            ).astype(jnp.bfloat16)
    acc_ref[...] = jnp.zeros(acc_ref.shape, jnp.float32)
    sides = []
    for cols in ((0, 1), (2, 3), (4, 5)):
        total = None
        for i in range(9):
            for half in range(2):
                term = jnp.dot(
                    w_ref[:, 512 * i + 256 * half : 512 * i + 256 * half + 256],
                    read_weights(halves[half], [1 + 6 * i + b for b in cols]),
                    preferred_element_type=jnp.float32,
                )
                total = term if total is None else total + term
        sides.append(total)
    sides.append(jnp.zeros((4 * ROWS, 128), jnp.float32))
    wide = jnp.concatenate(sides, 1)
    for c in range(4):
        first, off = divmod(720 * c, 128)
        block = wide[ROWS * c : ROWS * c + ROWS]
        if off:
            block = pltpu.roll(block, off, 1)
        span = pl.ds(128 * first, 896)
        acc_ref[:, span] = acc_ref[:, span] + block
    out_ref[...] = acc_ref[:, :D].reshape(out_ref.shape).astype(jnp.bfloat16)


def shards(trainer_flat, matching, prefix_kv, prefix_blocks, inputs):
    bf16, f32 = jnp.bfloat16, jnp.float32
    x = inputs[:, 0]
    prefix = prefix_kv[0]
    pair = lax.concatenate([prefix, lax.ppermute(prefix, AXES, Y_FAR)], 0)
    behind = lax.ppermute(pair, AXES, X_OUT)
    ahead = lax.ppermute(pair, AXES, X_BACK)
    across = lax.ppermute(behind, AXES, X_OUT)
    core_keys = lax.concatenate([pair, behind, ahead, across], 0)

    formed = pl.pallas_call(
        form_kernel,
        out_shape=jax.ShapeDtypeStruct((16, SLOT, 128), bf16),
        in_specs=[SMEM, VMEM],
        out_specs=VMEM,
        scratch_shapes=[pltpu.VMEM((64, 128), f32)],
        name="form",
    )(matching, trainer_flat)
    along_z = lax.all_to_all(formed, AXES, 0, 0, tiled=True, axis_index_groups=Z_GROUPS)
    merged = pl.pallas_call(
        merge_kernel,
        out_shape=jax.ShapeDtypeStruct((4, USED, 16, 128), bf16),
        in_specs=[VMEM],
        out_specs=VMEM,
        scratch_shapes=[pltpu.VMEM((16 * SLOT, 128), f32)],
        compiler_params=pltpu.CompilerParams(vmem_limit_bytes=8 * MIB),
        name="merge",
    )(along_z)
    lines = lax.all_to_all(merged, AXES, 0, 0, tiled=True, axis_index_groups=line_groups(0))
    lines, core_keys = lax.optimization_barrier((lines, core_keys))
    low = lax.ppermute(lines, AXES, RING_UP)
    high = lax.ppermute(lines, AXES, RING_DOWN)
    ends = lax.ppermute(lines, AXES, RING_FAR)
    x, _ = lax.optimization_barrier((inputs[:, 0], lines))
    gathered, places, out_rows = pl.pallas_call(
        pick_kernel,
        out_shape=(
            jax.ShapeDtypeStruct((11 * ROWS, 512), bf16),
            jax.ShapeDtypeStruct((1, 512), jnp.int32),
            jax.ShapeDtypeStruct((512, 512), bf16),
        ),
        in_specs=[VMEM] * 2,
        out_specs=(VMEM, VMEM, VMEM),
        scratch_shapes=[pltpu.VMEM((ROWS, 3072), f32), pltpu.VMEM((11 * ROWS, 3072), bf16)],
        compiler_params=pltpu.CompilerParams(vmem_limit_bytes=12 * MIB),
        name="pick",
    )(x, matching.reshape(1, 512))
    swapped, core_keys, _ = lax.optimization_barrier((lines, core_keys, gathered))
    other_lines = lax.ppermute(swapped, AXES, CORE_SWAP)
    other_keys = lax.ppermute(core_keys, AXES, CORE_SWAP)
    other_low = lax.ppermute(low, AXES, CORE_SWAP)
    other_high = lax.ppermute(high, AXES, CORE_SWAP)
    other_ends = lax.ppermute(ends, AXES, CORE_SWAP)
    mine = [lines, low, high, ends]
    other = [other_lines, other_low, other_high, other_ends]
    output = pl.pallas_call(
        tail_kernel,
        out_shape=jax.ShapeDtypeStruct(x.shape, bf16),
        in_specs=[SMEM] + [VMEM] * 13,
        out_specs=VMEM,
        scratch_shapes=[
            pltpu.VMEM((QHEADS * ROWS, 16 * SHARD), f32),
            pltpu.VMEM((4 * ROWS, 9 * 512), bf16),
            pltpu.VMEM((ROWS, 768), f32),
            pltpu.VMEM((ROWS, 3072), f32),
        ],
        compiler_params=pltpu.CompilerParams(vmem_limit_bytes=20 * MIB),
        name="tail",
    )(prefix_blocks, gathered, places, out_rows, *mine, *other, core_keys, other_keys)
    return output[:, None]


def solution(mesh):
    in_specs = (
        P(("group", "sample"), None),
        P(),
        P("group", "sample", None),
        P("group"),
        P(None, "group", "sample", None),
    )
    out_specs = P(None, "group", "sample", None)
    return jax.shard_map(shards, mesh=mesh, in_specs=in_specs, out_specs=out_specs, check_vma=False)
```

```python
import functools

import jax
import jax.numpy as jnp
import numpy as np
from jax import lax
from jax.experimental import pallas as pl
from jax.experimental.pallas import tpu as pltpu
from jax.sharding import PartitionSpec as P

D = 2880
HEAD = 64
QHEADS = 8
AXES = ("group", "sample")
TILE = 6480
IN_ROWS = 2880
IN_SIZE = 2880 * 640
SLOT = 56
USED = 55
ROWS = 32
VMEM = pl.BlockSpec(memory_space=pltpu.VMEM)
SMEM = pl.BlockSpec(memory_space=pltpu.SMEM)
MIB = 1024 * 1024


def device_id(z, y, x, core):
    return z * 32 + (y % 2) * 16 + (y // 2) * 8 + x * 2 + core


Z_GROUPS = [
    [device_id(z, y, x, c) for z in range(16)] for y in range(4) for x in range(4) for c in range(2)
]


def line_groups(x_core):
    along_x = [[device_id(z, y, x, x_core) for x in range(4)] for z in range(16) for y in range(4)]
    along_y = [
        [device_id(z, y, x, 1 - x_core) for y in range(4)] for z in range(16) for x in range(4)
    ]
    return along_x + along_y


def moves(step):
    pairs = []
    for z in range(16):
        for y in range(4):
            for x in range(4):
                for c in range(2):
                    y2, x2, c2 = step(y, x, c)
                    pairs.append((device_id(z, y, x, c), device_id(z, y2 % 4, x2 % 4, c2)))
    return pairs


CORE_SWAP = moves(lambda y, x, c: (y, x, 1 - c))
X_OUT = moves(lambda y, x, c: (y, x - 1 if c else x + 1, c))
X_BACK = moves(lambda y, x, c: (y, x + 1 if c else x - 1, c))
Y_FAR = moves(lambda y, x, c: (y + 2, x, c))
RING_UP = moves(lambda y, x, c: (y, x + 1, c) if c else (y + 1, x, c))
RING_FAR = moves(lambda y, x, c: (y, x + 2, c) if c else (y + 2, x, c))
RING_DOWN = moves(lambda y, x, c: (y, x - 1, c) if c else (y - 1, x, c))


def form_kernel(matching_ref, tile_ref, out_ref, buf_ref):
    me = lax.axis_index("group") * 16 + lax.axis_index("sample")
    place = matching_ref[me]
    buf_ref[...] = jnp.zeros((64, 128), jnp.float32)
    for r in range(50):
        buf_ref[r : r + 1, :] = tile_ref[:, 128 * r : 128 * r + 128].astype(jnp.float32)
    buf_ref[50:51, :80] = tile_ref[:, 6400:6480].astype(jnp.float32)
    raw = buf_ref[...]
    row = lax.broadcasted_iota(jnp.int32, (64, 128), 0)
    lane = lax.broadcasted_iota(jnp.int32, (64, 128), 1)
    in_len = jnp.clip(IN_SIZE - TILE * place, 0, TILE)
    part = jnp.where(row * 128 + lane < in_len, raw, 0.0)
    shift = 80 * (place & 7)
    lanes = shift & 127
    turned = pltpu.roll(part, lanes, 1)
    above = pltpu.roll(turned, 1, 0)
    shifted = pltpu.roll(jnp.where(lane >= lanes, turned, above), shift >> 7, 0)
    units = []
    lane8 = lax.broadcasted_iota(jnp.int32, (8, 128), 1)
    row8 = lax.broadcasted_iota(jnp.int32, (8, 128), 0)
    for i in range(9):
        base, off = divmod(720 * i, 128)
        window = buf_ref[base : base + 8, :]
        if off:
            window = pltpu.roll(window, 128 - off, 1)
            below = pltpu.roll(window, 7, 0)
            window = jnp.where(lane8 < 128 - off, window, below)
        units.append(jnp.where((row8 < 5) | (lane8 < 80), window, 0.0)[:6])
    for i in range(9):
        buf_ref[1 + 6 * i : 7 + 6 * i, :] = units[i]
    first = 1 + 6 * jnp.clip(2560 - 9 * place, 0, 9)
    out = jnp.where((row >= first) & (row < 55), buf_ref[...], 0.0) + shifted
    out = out[:SLOT].astype(jnp.bfloat16)
    for j in range(out_ref.shape[0]):
        out_ref[j] = out


def merge_kernel(in_ref, out_ref, buf_ref):
    for j in range(16):
        buf_ref[SLOT * j : SLOT * j + SLOT, :] = in_ref[j].astype(jnp.float32)
    for r in range(USED):
        low = buf_ref[pl.ds(r, 8, stride=SLOT), :]
        high = buf_ref[pl.ds(r + 8 * SLOT, 8, stride=SLOT), :]
        both = jnp.concatenate([low, high], 0).astype(jnp.bfloat16)
        for k in range(out_ref.shape[0]):
            out_ref[k, r] = both


def read_weights(refs, rows):
    columns = []
    for r in rows:
        columns.append(jnp.concatenate([ref[:, r].reshape(-1, 128) for ref in refs], 0))
    return jnp.concatenate(columns, 1)


def chip_place():
    group, sample = lax.axis_index("group"), lax.axis_index("sample")
    core = sample & 1
    x = (sample >> 1) & 3
    y = (sample >> 3) * 2 + (group & 1)
    return y, x, core


def ring_offset(piece):
    return jnp.where(piece == 0, 0, jnp.where(piece == 3, 1, piece + 1))


def slot_places(matching_row):
    y0, x0, core0 = chip_place()
    slot = lax.broadcasted_iota(jnp.int32, (1, 512), 1)
    core = core0 ^ (slot >> 8)
    offset = ring_offset((slot >> 6) & 3)
    line = (slot >> 4) & 3
    y = jnp.where(core == 0, (y0 + offset) & 3, line)
    x = jnp.where(core == 0, line, (x0 + offset) & 3)
    device = (slot & 15) * 32 + (y & 1) * 16 + (y >> 1) * 8 + x * 2 + core
    rows = lax.broadcasted_iota(jnp.int32, (512, 512), 0)
    chosen = jnp.where(rows == device, 1.0, 0.0).astype(jnp.bfloat16)
    row = lax.broadcasted_iota(jnp.int32, (8, 512), 0)
    digits = jnp.where(row == 0, matching_row >> 4, jnp.where(row == 1, matching_row & 15, 0))
    picked = jnp.dot(
        digits.astype(jnp.float32).astype(jnp.bfloat16), chosen, preferred_element_type=jnp.float32
    ).astype(jnp.int32)
    return picked[0:1] * 16 + picked[1:2]


def pick_kernel(x_ref, matching_ref, xg_ref, place_ref, row_ref, xs_ref, a_ref):
    place = slot_places(matching_ref[...])
    place_ref[...] = place
    row = jnp.where(place >= 284, ((9 * place - 2560) >> 2) + 1, -1)
    row_ref[...] = jnp.where(
        lax.broadcasted_iota(jnp.int32, (512, 512), 0) == row, 1.0, 0.0
    ).astype(jnp.bfloat16)
    xs_ref[:, 2816:] = jnp.zeros((ROWS, 256), jnp.float32)
    xs_ref[:, :D] = x_ref[...].astype(jnp.float32).reshape(ROWS, D)
    xs = xs_ref[...]
    for i in range(11):
        moved = xs if i == 0 else pltpu.roll(xs, 3072 - i, 1)
        a_ref[ROWS * i : ROWS * i + ROWS, :] = moved.astype(jnp.bfloat16)
    start = jnp.where(place <= 284, 10 * place + (place >> 3), -1)
    total = None
    for k in range(12):
        rows = lax.broadcasted_iota(jnp.int32, (256, 512), 0) + 256 * k
        chosen = jnp.where(rows == start, 1.0, 0.0).astype(jnp.bfloat16)
        term = jnp.dot(
            a_ref[:, 256 * k : 256 * k + 256], chosen, preferred_element_type=jnp.float32
        )
        total = term if total is None else total + term
    xg_ref[...] = total.astype(jnp.bfloat16)


def project(xg_ref, halves, first):
    blocks = []
    for cols in ((0, 1), (2, 3), (4,)):
        total = None
        for half in range(2):
            slots = slice(256 * half + first, 256 * half + first + 128)
            for i in range(11):
                term = jnp.dot(
                    xg_ref[ROWS * i : ROWS * i + ROWS, slots],
                    read_weights(halves[half], [5 * i + b for b in cols]),
                    preferred_element_type=jnp.float32,
                )
                total = term if total is None else total + term
        blocks.append(total)
    return jnp.concatenate(blocks, 1)


def early_kernel(xg_ref, m0, m1, o0, o1, out_ref):
    out_ref[...] = project(xg_ref, ((m0, m1), (o0, o1)), 0)


CHUNK = 1024
SHARD = 512


def tail_kernel(
    limit_ref, part_ref, xg_ref, place_ref, row_ref, m0, m1, m2, m3, o0, o1, o2, o3, near_ref, far_ref, out_ref,
    s_ref, w_ref, og_ref, acc_ref,
):
    halves = ((m0, m1, m2, m3), (o0, o1, o2, o3))
    projected = part_ref[...] + project(xg_ref, ((m2, m3), (o2, o3)), 128)
    y0, x0, core0 = chip_place()
    rounded = projected.astype(jnp.bfloat16)
    own_kv = rounded[:, 512:640]
    heads = []
    zero = jnp.zeros((ROWS, HEAD), jnp.float32)
    for h in range(QHEADS):
        heads.append(jnp.concatenate([projected[:, HEAD * h : HEAD * h + HEAD], zero], 1))
    query = jnp.concatenate(heads, 0).astype(jnp.bfloat16)
    count = QHEADS * ROWS
    scale = np.float32(HEAD**-0.5 * np.log2(np.e))
    contract = (((1,), (1,)), ((), ()))
    limit = limit_ref[0] * 128

    own = lax.dot_general(query, own_kv, contract, preferred_element_type=jnp.float32)
    row = lax.broadcasted_iota(jnp.int32, (count, ROWS), 0)
    col = lax.broadcasted_iota(jnp.int32, (count, ROWS), 1)
    allowed = ((row & 7) == (col & 7)) & ((col >> 3) <= ((row >> 3) & 3))
    own = jnp.where(allowed, own, -1e30)

    chunks = 16 * SHARD // CHUNK
    def read_keys(k):
        ref = near_ref if k < chunks // 2 else far_ref
        first = CHUNK * (k % (chunks // 2))
        return ref[first : first + CHUNK, :]

    peak = jnp.full((count, 128), -1e30, jnp.float32)
    for k in range(chunks):
        scores = lax.dot_general(
            query, read_keys(k), contract, preferred_element_type=jnp.float32
        )
        bias = []
        for n in range(CHUNK // SHARD * k, CHUNK // SHARD * (k + 1)):
            core = core0 ^ (n >> 3)
            offset = (0, 3 - 2 * core, 1 + 2 * core, 2)[(n >> 1) & 3]
            shard = ((y0 >> 1) ^ (n & 1)) * 8 + ((x0 + offset) & 3) * 2 + core
            keys = lax.broadcasted_iota(jnp.int32, (1, SHARD), 1)
            bias.append(jnp.where(keys < limit - SHARD * shard, 0.0, -1e30))
        scores = scores + jnp.concatenate(bias, 1)
        s_ref[:, CHUNK * k : CHUNK * k + CHUNK] = scores
        for n in range(CHUNK // 128):
            peak = jnp.maximum(peak, scores[:, 128 * n : 128 * n + 128])
    top = jnp.maximum(jnp.max(peak, 1, keepdims=True), jnp.max(own, 1, keepdims=True))
    floor = top * scale

    lane = lax.broadcasted_iota(jnp.int32, (1, 128), 1)
    kept = jnp.where(lane < HEAD, 0.0, 1.0).astype(jnp.bfloat16)
    ones = jnp.where(lane < HEAD, 1.0, 0.0).astype(jnp.bfloat16)

    def with_ones(piece):
        return piece * kept + ones

    weights = jnp.where(allowed, jnp.exp2(own * scale - floor), 0.0).astype(jnp.bfloat16)
    summed = jnp.dot(weights, with_ones(own_kv), preferred_element_type=jnp.float32)
    for k in range(chunks):
        powers = s_ref[:, CHUNK * k : CHUNK * k + CHUNK] * scale - floor
        weights = jnp.exp2(powers.astype(jnp.bfloat16))
        summed = summed + jnp.dot(
            weights,
            with_ones(read_keys(k)),
            preferred_element_type=jnp.float32,
        )
    mixed = summed[:, HEAD:] / summed[:, :HEAD]
    og_ref[...] = jnp.zeros(og_ref.shape, jnp.float32)
    for h in range(QHEADS):
        og_ref[:, 128 + HEAD * h : 128 + HEAD * h + HEAD] = mixed[ROWS * h : ROWS * h + ROWS]

    place = place_ref[...]
    unit = 9 * place - 2560
    padded = og_ref[...]
    moved = [
        pltpu.roll(padded, 1, 1)[:, 128:640],
        padded[:, 128:640],
        pltpu.roll(padded, 767, 1)[:, 128:640],
    ]
    stacked = jnp.concatenate(moved, 0).astype(jnp.bfloat16)
    picked = jnp.dot(stacked, row_ref[...], preferred_element_type=jnp.float32)
    phase = unit & 3
    for i in range(9):
        for c in range(4):
            wanted = (c - i) % 4
            d = (wanted + i) // 4
            w_ref[ROWS * c : ROWS * c + ROWS, 512 * i : 512 * i + 512] = jnp.where(
                phase == wanted, picked[ROWS * d : ROWS * d + ROWS], 0.0
            ).astype(jnp.bfloat16)
    acc_ref[...] = jnp.zeros(acc_ref.shape, jnp.float32)
    sides = []
    for cols in ((0, 1), (2, 3), (4, 5)):
        total = None
        for i in range(9):
            for half in range(2):
                term = jnp.dot(
                    w_ref[:, 512 * i + 256 * half : 512 * i + 256 * half + 256],
                    read_weights(halves[half], [1 + 6 * i + b for b in cols]),
                    preferred_element_type=jnp.float32,
                )
                total = term if total is None else total + term
        sides.append(total)
    sides.append(jnp.zeros((4 * ROWS, 128), jnp.float32))
    wide = jnp.concatenate(sides, 1)
    for c in range(4):
        first, off = divmod(720 * c, 128)
        block = wide[ROWS * c : ROWS * c + ROWS]
        if off:
            block = pltpu.roll(block, off, 1)
        span = pl.ds(128 * first, 896)
        acc_ref[:, span] = acc_ref[:, span] + block
    out_ref[...] = acc_ref[:, :D].reshape(out_ref.shape).astype(jnp.bfloat16)


def shards(trainer_flat, matching, prefix_kv, prefix_blocks, inputs):
    bf16, f32 = jnp.bfloat16, jnp.float32
    x = inputs[:, 0]
    prefix = prefix_kv[0]
    pair = lax.concatenate([prefix, lax.ppermute(prefix, AXES, Y_FAR)], 0)
    behind = lax.ppermute(pair, AXES, X_OUT)
    ahead = lax.ppermute(pair, AXES, X_BACK)
    across = lax.ppermute(behind, AXES, X_OUT)
    core_keys = lax.concatenate([pair, behind, ahead, across], 0)

    formed = pl.pallas_call(
        form_kernel,
        out_shape=jax.ShapeDtypeStruct((16, SLOT, 128), bf16),
        in_specs=[SMEM, VMEM],
        out_specs=VMEM,
        scratch_shapes=[pltpu.VMEM((64, 128), f32)],
        name="form",
    )(matching, trainer_flat)
    along_z = lax.all_to_all(formed, AXES, 0, 0, tiled=True, axis_index_groups=Z_GROUPS)
    merged = pl.pallas_call(
        merge_kernel,
        out_shape=jax.ShapeDtypeStruct((4, USED, 16, 128), bf16),
        in_specs=[VMEM],
        out_specs=VMEM,
        scratch_shapes=[pltpu.VMEM((16 * SLOT, 128), f32)],
        compiler_params=pltpu.CompilerParams(vmem_limit_bytes=8 * MIB),
        name="merge",
    )(along_z)
    lines = lax.all_to_all(merged, AXES, 0, 0, tiled=True, axis_index_groups=line_groups(0))
    lines, core_keys = lax.optimization_barrier((lines, core_keys))
    low = lax.ppermute(lines, AXES, RING_UP)
    high = lax.ppermute(lines, AXES, RING_DOWN)
    ends = lax.ppermute(lines, AXES, RING_FAR)
    x, _ = lax.optimization_barrier((inputs[:, 0], lines))
    gathered, places, out_rows = pl.pallas_call(
        pick_kernel,
        out_shape=(
            jax.ShapeDtypeStruct((11 * ROWS, 512), bf16),
            jax.ShapeDtypeStruct((1, 512), jnp.int32),
            jax.ShapeDtypeStruct((512, 512), bf16),
        ),
        in_specs=[VMEM] * 2,
        out_specs=(VMEM, VMEM, VMEM),
        scratch_shapes=[pltpu.VMEM((ROWS, 3072), f32), pltpu.VMEM((11 * ROWS, 3072), bf16)],
        compiler_params=pltpu.CompilerParams(vmem_limit_bytes=12 * MIB),
        name="pick",
    )(x, matching.reshape(1, 512))
    swapped, core_keys, _ = lax.optimization_barrier((lines, core_keys, gathered))
    other_lines = lax.ppermute(swapped, AXES, CORE_SWAP)
    other_keys = lax.ppermute(core_keys, AXES, CORE_SWAP)
    other_low = lax.ppermute(low, AXES, CORE_SWAP)
    other_ends = lax.ppermute(ends, AXES, CORE_SWAP)
    part = pl.pallas_call(
        early_kernel,
        out_shape=jax.ShapeDtypeStruct((ROWS, 640), f32),
        in_specs=[VMEM] * 5,
        out_specs=VMEM,
        compiler_params=pltpu.CompilerParams(vmem_limit_bytes=8 * MIB),
        name="early",
    )(gathered, lines, ends, other_lines, other_ends)
    other_high = lax.ppermute(high, AXES, CORE_SWAP)
    mine = [lines, ends, low, high]
    other = [other_lines, other_ends, other_low, other_high]
    output = pl.pallas_call(
        tail_kernel,
        out_shape=jax.ShapeDtypeStruct(x.shape, bf16),
        in_specs=[SMEM] + [VMEM] * 14,
        out_specs=VMEM,
        scratch_shapes=[
            pltpu.VMEM((QHEADS * ROWS, 16 * SHARD), f32),
            pltpu.VMEM((4 * ROWS, 9 * 512), bf16),
            pltpu.VMEM((ROWS, 768), f32),
            pltpu.VMEM((ROWS, 3072), f32),
        ],
        compiler_params=pltpu.CompilerParams(vmem_limit_bytes=20 * MIB),
        name="tail",
    )(prefix_blocks, part, gathered, places, out_rows, *mine, *other, core_keys, other_keys)
    return output[:, None]


def solution(mesh):
    in_specs = (
        P(("group", "sample"), None),
        P(),
        P("group", "sample", None),
        P("group"),
        P(None, "group", "sample", None),
    )
    out_specs = P(None, "group", "sample", None)
    return jax.shard_map(shards, mesh=mesh, in_specs=in_specs, out_specs=out_specs, check_vma=False)
```

```python
import functools

import jax
import jax.numpy as jnp
import numpy as np
from jax import lax
from jax.experimental import pallas as pl
from jax.experimental.pallas import tpu as pltpu
from jax.sharding import PartitionSpec as P

D = 2880
HEAD = 64
QHEADS = 8
AXES = ("group", "sample")
TILE = 6480
IN_ROWS = 2880
IN_SIZE = 2880 * 640
SLOT = 56
USED = 55
ROWS = 32
VMEM = pl.BlockSpec(memory_space=pltpu.VMEM)
SMEM = pl.BlockSpec(memory_space=pltpu.SMEM)
MIB = 1024 * 1024


def device_id(z, y, x, core):
    return z * 32 + (y % 2) * 16 + (y // 2) * 8 + x * 2 + core


Z_GROUPS = [
    [device_id(z, y, x, c) for z in range(16)] for y in range(4) for x in range(4) for c in range(2)
]


def line_groups(x_core):
    along_x = [[device_id(z, y, x, x_core) for x in range(4)] for z in range(16) for y in range(4)]
    along_y = [
        [device_id(z, y, x, 1 - x_core) for y in range(4)] for z in range(16) for x in range(4)
    ]
    return along_x + along_y


def moves(step):
    pairs = []
    for z in range(16):
        for y in range(4):
            for x in range(4):
                for c in range(2):
                    y2, x2, c2 = step(y, x, c)
                    pairs.append((device_id(z, y, x, c), device_id(z, y2 % 4, x2 % 4, c2)))
    return pairs


CORE_SWAP = moves(lambda y, x, c: (y, x, 1 - c))
X_OUT = moves(lambda y, x, c: (y, x - 1 if c else x + 1, c))
X_BACK = moves(lambda y, x, c: (y, x + 1 if c else x - 1, c))
Y_FAR = moves(lambda y, x, c: (y + 2, x, c))
RING_UP = moves(lambda y, x, c: (y, x + 1, c) if c else (y + 1, x, c))
RING_FAR = moves(lambda y, x, c: (y, x + 2, c) if c else (y + 2, x, c))
RING_DOWN = moves(lambda y, x, c: (y, x - 1, c) if c else (y - 1, x, c))


def form_kernel(matching_ref, tile_ref, out_ref, buf_ref):
    me = lax.axis_index("group") * 16 + lax.axis_index("sample")
    place = matching_ref[me]
    buf_ref[...] = jnp.zeros((64, 128), jnp.float32)
    for r in range(50):
        buf_ref[r : r + 1, :] = tile_ref[:, 128 * r : 128 * r + 128].astype(jnp.float32)
    buf_ref[50:51, :80] = tile_ref[:, 6400:6480].astype(jnp.float32)
    raw = buf_ref[...]
    row = lax.broadcasted_iota(jnp.int32, (64, 128), 0)
    lane = lax.broadcasted_iota(jnp.int32, (64, 128), 1)
    in_len = jnp.clip(IN_SIZE - TILE * place, 0, TILE)
    part = jnp.where(row * 128 + lane < in_len, raw, 0.0)
    shift = 80 * (place & 7)
    lanes = shift & 127
    turned = pltpu.roll(part, lanes, 1)
    above = pltpu.roll(turned, 1, 0)
    shifted = pltpu.roll(jnp.where(lane >= lanes, turned, above), shift >> 7, 0)
    units = []
    lane8 = lax.broadcasted_iota(jnp.int32, (8, 128), 1)
    row8 = lax.broadcasted_iota(jnp.int32, (8, 128), 0)
    for i in range(9):
        base, off = divmod(720 * i, 128)
        window = buf_ref[base : base + 8, :]
        if off:
            window = pltpu.roll(window, 128 - off, 1)
            below = pltpu.roll(window, 7, 0)
            window = jnp.where(lane8 < 128 - off, window, below)
        units.append(jnp.where((row8 < 5) | (lane8 < 80), window, 0.0)[:6])
    for i in range(9):
        buf_ref[1 + 6 * i : 7 + 6 * i, :] = units[i]
    first = 1 + 6 * jnp.clip(2560 - 9 * place, 0, 9)
    out = jnp.where((row >= first) & (row < 55), buf_ref[...], 0.0) + shifted
    out = out[:SLOT].astype(jnp.bfloat16)
    for j in range(out_ref.shape[0]):
        out_ref[j] = out


def merge_kernel(in_ref, out_ref, buf_ref):
    for j in range(16):
        buf_ref[SLOT * j : SLOT * j + SLOT, :] = in_ref[j].astype(jnp.float32)
    for r in range(USED):
        low = buf_ref[pl.ds(r, 8, stride=SLOT), :]
        high = buf_ref[pl.ds(r + 8 * SLOT, 8, stride=SLOT), :]
        both = jnp.concatenate([low, high], 0).astype(jnp.bfloat16)
        for k in range(out_ref.shape[0]):
            out_ref[k, r] = both


def read_weights(refs, rows):
    columns = []
    for r in rows:
        columns.append(jnp.concatenate([ref[:, r].reshape(-1, 128) for ref in refs], 0))
    return jnp.concatenate(columns, 1)


def chip_place():
    group, sample = lax.axis_index("group"), lax.axis_index("sample")
    core = sample & 1
    x = (sample >> 1) & 3
    y = (sample >> 3) * 2 + (group & 1)
    return y, x, core


def ring_offset(piece):
    return jnp.where(piece == 0, 0, jnp.where(piece == 3, 1, piece + 1))


def slot_places(matching_row):
    y0, x0, core0 = chip_place()
    slot = lax.broadcasted_iota(jnp.int32, (1, 512), 1)
    core = core0 ^ (slot >> 8)
    offset = ring_offset((slot >> 6) & 3)
    line = (slot >> 4) & 3
    y = jnp.where(core == 0, (y0 + offset) & 3, line)
    x = jnp.where(core == 0, line, (x0 + offset) & 3)
    device = (slot & 15) * 32 + (y & 1) * 16 + (y >> 1) * 8 + x * 2 + core
    rows = lax.broadcasted_iota(jnp.int32, (512, 512), 0)
    chosen = jnp.where(rows == device, 1.0, 0.0).astype(jnp.bfloat16)
    row = lax.broadcasted_iota(jnp.int32, (8, 512), 0)
    digits = jnp.where(row == 0, matching_row >> 4, jnp.where(row == 1, matching_row & 15, 0))
    picked = jnp.dot(
        digits.astype(jnp.float32).astype(jnp.bfloat16), chosen, preferred_element_type=jnp.float32
    ).astype(jnp.int32)
    return picked[0:1] * 16 + picked[1:2]


def pick_kernel(x_ref, matching_ref, xg_ref, place_ref, row_ref, xs_ref, a_ref):
    place = slot_places(matching_ref[...])
    place_ref[...] = place
    row = jnp.where(place >= 284, ((9 * place - 2560) >> 2) + 1, -1)
    row_ref[...] = jnp.where(
        lax.broadcasted_iota(jnp.int32, (512, 512), 0) == row, 1.0, 0.0
    ).astype(jnp.bfloat16)
    xs_ref[:, 2816:] = jnp.zeros((ROWS, 256), jnp.float32)
    xs_ref[:, :D] = x_ref[...].astype(jnp.float32).reshape(ROWS, D)
    xs = xs_ref[...]
    for i in range(11):
        moved = xs if i == 0 else pltpu.roll(xs, 3072 - i, 1)
        a_ref[ROWS * i : ROWS * i + ROWS, :] = moved.astype(jnp.bfloat16)
    start = jnp.where(place <= 284, 10 * place + (place >> 3), -1)
    total = None
    for k in range(12):
        rows = lax.broadcasted_iota(jnp.int32, (256, 512), 0) + 256 * k
        chosen = jnp.where(rows == start, 1.0, 0.0).astype(jnp.bfloat16)
        term = jnp.dot(
            a_ref[:, 256 * k : 256 * k + 256], chosen, preferred_element_type=jnp.float32
        )
        total = term if total is None else total + term
    xg_ref[...] = total.astype(jnp.bfloat16)


def project(xg_ref, groups):
    blocks = []
    for cols in ((0, 1), (2, 3), (4,)):
        total = None
        for refs, slots in groups:
            for i in range(11):
                term = jnp.dot(
                    xg_ref[ROWS * i : ROWS * i + ROWS, slots],
                    read_weights(refs, [5 * i + b for b in cols]),
                    preferred_element_type=jnp.float32,
                )
                total = term if total is None else total + term
        blocks.append(total)
    return jnp.concatenate(blocks, 1)


def early_kernel(xg_ref, m0, m1, m2, m3, o0, o1, out_ref):
    groups = (((m0, m1, m2, m3), slice(0, 256)), ((o0, o1), slice(256, 384)))
    out_ref[...] = project(xg_ref, groups)


CHUNK = 1024
SHARD = 512


def tail_kernel(
    limit_ref, part_ref, xg_ref, place_ref, row_ref, m0, m1, m2, m3, o0, o1, o2, o3, near_ref, far_ref, out_ref,
    s_ref, w_ref, og_ref, acc_ref,
):
    halves = ((m0, m1, m2, m3), (o0, o1, o2, o3))
    projected = part_ref[...] + project(xg_ref, (((o2, o3), slice(384, 512)),))
    y0, x0, core0 = chip_place()
    rounded = projected.astype(jnp.bfloat16)
    own_kv = rounded[:, 512:640]
    heads = []
    zero = jnp.zeros((ROWS, HEAD), jnp.float32)
    for h in range(QHEADS):
        heads.append(jnp.concatenate([projected[:, HEAD * h : HEAD * h + HEAD], zero], 1))
    query = jnp.concatenate(heads, 0).astype(jnp.bfloat16)
    count = QHEADS * ROWS
    scale = np.float32(HEAD**-0.5 * np.log2(np.e))
    contract = (((1,), (1,)), ((), ()))
    limit = limit_ref[0] * 128

    own = lax.dot_general(query, own_kv, contract, preferred_element_type=jnp.float32)
    row = lax.broadcasted_iota(jnp.int32, (count, ROWS), 0)
    col = lax.broadcasted_iota(jnp.int32, (count, ROWS), 1)
    allowed = ((row & 7) == (col & 7)) & ((col >> 3) <= ((row >> 3) & 3))
    own = jnp.where(allowed, own, -1e30)

    chunks = 16 * SHARD // CHUNK
    def read_keys(k):
        ref = near_ref if k < chunks // 2 else far_ref
        first = CHUNK * (k % (chunks // 2))
        return ref[first : first + CHUNK, :]

    peak = jnp.full((count, 128), -1e30, jnp.float32)
    for k in range(chunks):
        scores = lax.dot_general(
            query, read_keys(k), contract, preferred_element_type=jnp.float32
        )
        bias = []
        for n in range(CHUNK // SHARD * k, CHUNK // SHARD * (k + 1)):
            core = core0 ^ (n >> 3)
            offset = (0, 3 - 2 * core, 1 + 2 * core, 2)[(n >> 1) & 3]
            shard = ((y0 >> 1) ^ (n & 1)) * 8 + ((x0 + offset) & 3) * 2 + core
            keys = lax.broadcasted_iota(jnp.int32, (1, SHARD), 1)
            bias.append(jnp.where(keys < limit - SHARD * shard, 0.0, -1e30))
        scores = scores + jnp.concatenate(bias, 1)
        s_ref[:, CHUNK * k : CHUNK * k + CHUNK] = scores
        for n in range(CHUNK // 128):
            peak = jnp.maximum(peak, scores[:, 128 * n : 128 * n + 128])
    top = jnp.maximum(jnp.max(peak, 1, keepdims=True), jnp.max(own, 1, keepdims=True))
    floor = top * scale

    lane = lax.broadcasted_iota(jnp.int32, (1, 128), 1)
    kept = jnp.where(lane < HEAD, 0.0, 1.0).astype(jnp.bfloat16)
    ones = jnp.where(lane < HEAD, 1.0, 0.0).astype(jnp.bfloat16)

    def with_ones(piece):
        return piece * kept + ones

    weights = jnp.where(allowed, jnp.exp2(own * scale - floor), 0.0).astype(jnp.bfloat16)
    summed = jnp.dot(weights, with_ones(own_kv), preferred_element_type=jnp.float32)
    for k in range(chunks):
        powers = s_ref[:, CHUNK * k : CHUNK * k + CHUNK] * scale - floor
        weights = jnp.exp2(powers.astype(jnp.bfloat16))
        summed = summed + jnp.dot(
            weights,
            with_ones(read_keys(k)),
            preferred_element_type=jnp.float32,
        )
    mixed = summed[:, HEAD:] / summed[:, :HEAD]
    og_ref[...] = jnp.zeros(og_ref.shape, jnp.float32)
    for h in range(QHEADS):
        og_ref[:, 128 + HEAD * h : 128 + HEAD * h + HEAD] = mixed[ROWS * h : ROWS * h + ROWS]

    place = place_ref[...]
    unit = 9 * place - 2560
    padded = og_ref[...]
    moved = [
        pltpu.roll(padded, 1, 1)[:, 128:640],
        padded[:, 128:640],
        pltpu.roll(padded, 767, 1)[:, 128:640],
    ]
    stacked = jnp.concatenate(moved, 0).astype(jnp.bfloat16)
    picked = jnp.dot(stacked, row_ref[...], preferred_element_type=jnp.float32)
    phase = unit & 3
    for i in range(9):
        for c in range(4):
            wanted = (c - i) % 4
            d = (wanted + i) // 4
            w_ref[ROWS * c : ROWS * c + ROWS, 512 * i : 512 * i + 512] = jnp.where(
                phase == wanted, picked[ROWS * d : ROWS * d + ROWS], 0.0
            ).astype(jnp.bfloat16)
    acc_ref[...] = jnp.zeros(acc_ref.shape, jnp.float32)
    sides = []
    for cols in ((0, 1), (2, 3), (4, 5)):
        total = None
        for i in range(9):
            for half in range(2):
                term = jnp.dot(
                    w_ref[:, 512 * i + 256 * half : 512 * i + 256 * half + 256],
                    read_weights(halves[half], [1 + 6 * i + b for b in cols]),
                    preferred_element_type=jnp.float32,
                )
                total = term if total is None else total + term
        sides.append(total)
    sides.append(jnp.zeros((4 * ROWS, 128), jnp.float32))
    wide = jnp.concatenate(sides, 1)
    for c in range(4):
        first, off = divmod(720 * c, 128)
        block = wide[ROWS * c : ROWS * c + ROWS]
        if off:
            block = pltpu.roll(block, off, 1)
        span = pl.ds(128 * first, 896)
        acc_ref[:, span] = acc_ref[:, span] + block
    out_ref[...] = acc_ref[:, :D].reshape(out_ref.shape).astype(jnp.bfloat16)


def shards(trainer_flat, matching, prefix_kv, prefix_blocks, inputs):
    bf16, f32 = jnp.bfloat16, jnp.float32
    x = inputs[:, 0]
    prefix = prefix_kv[0]
    pair = lax.concatenate([prefix, lax.ppermute(prefix, AXES, Y_FAR)], 0)
    behind = lax.ppermute(pair, AXES, X_OUT)
    ahead = lax.ppermute(pair, AXES, X_BACK)
    across = lax.ppermute(behind, AXES, X_OUT)
    core_keys = lax.concatenate([pair, behind, ahead, across], 0)

    formed = pl.pallas_call(
        form_kernel,
        out_shape=jax.ShapeDtypeStruct((16, SLOT, 128), bf16),
        in_specs=[SMEM, VMEM],
        out_specs=VMEM,
        scratch_shapes=[pltpu.VMEM((64, 128), f32)],
        name="form",
    )(matching, trainer_flat)
    along_z = lax.all_to_all(formed, AXES, 0, 0, tiled=True, axis_index_groups=Z_GROUPS)
    merged = pl.pallas_call(
        merge_kernel,
        out_shape=jax.ShapeDtypeStruct((4, USED, 16, 128), bf16),
        in_specs=[VMEM],
        out_specs=VMEM,
        scratch_shapes=[pltpu.VMEM((16 * SLOT, 128), f32)],
        compiler_params=pltpu.CompilerParams(vmem_limit_bytes=8 * MIB),
        name="merge",
    )(along_z)
    lines = lax.all_to_all(merged, AXES, 0, 0, tiled=True, axis_index_groups=line_groups(0))
    lines, core_keys = lax.optimization_barrier((lines, core_keys))
    low = lax.ppermute(lines, AXES, RING_UP)
    high = lax.ppermute(lines, AXES, RING_DOWN)
    ends = lax.ppermute(lines, AXES, RING_FAR)
    x, _ = lax.optimization_barrier((inputs[:, 0], lines))
    gathered, places, out_rows = pl.pallas_call(
        pick_kernel,
        out_shape=(
            jax.ShapeDtypeStruct((11 * ROWS, 512), bf16),
            jax.ShapeDtypeStruct((1, 512), jnp.int32),
            jax.ShapeDtypeStruct((512, 512), bf16),
        ),
        in_specs=[VMEM] * 2,
        out_specs=(VMEM, VMEM, VMEM),
        scratch_shapes=[pltpu.VMEM((ROWS, 3072), f32), pltpu.VMEM((11 * ROWS, 3072), bf16)],
        compiler_params=pltpu.CompilerParams(vmem_limit_bytes=12 * MIB),
        name="pick",
    )(x, matching.reshape(1, 512))
    swapped, core_keys, _ = lax.optimization_barrier((lines, core_keys, gathered))
    other_lines = lax.ppermute(swapped, AXES, CORE_SWAP)
    other_keys = lax.ppermute(core_keys, AXES, CORE_SWAP)
    other_low = lax.ppermute(low, AXES, CORE_SWAP)
    other_ends = lax.ppermute(ends, AXES, CORE_SWAP)
    part = pl.pallas_call(
        early_kernel,
        out_shape=jax.ShapeDtypeStruct((ROWS, 640), f32),
        in_specs=[VMEM] * 7,
        out_specs=VMEM,
        compiler_params=pltpu.CompilerParams(vmem_limit_bytes=8 * MIB),
        name="early",
    )(gathered, lines, ends, low, high, other_lines, other_ends)
    other_high = lax.ppermute(high, AXES, CORE_SWAP)
    mine = [lines, ends, low, high]
    other = [other_lines, other_ends, other_low, other_high]
    output = pl.pallas_call(
        tail_kernel,
        out_shape=jax.ShapeDtypeStruct(x.shape, bf16),
        in_specs=[SMEM] + [VMEM] * 14,
        out_specs=VMEM,
        scratch_shapes=[
            pltpu.VMEM((QHEADS * ROWS, 16 * SHARD), f32),
            pltpu.VMEM((4 * ROWS, 9 * 512), bf16),
            pltpu.VMEM((ROWS, 768), f32),
            pltpu.VMEM((ROWS, 3072), f32),
        ],
        compiler_params=pltpu.CompilerParams(vmem_limit_bytes=20 * MIB),
        name="tail",
    )(prefix_blocks, part, gathered, places, out_rows, *mine, *other, core_keys, other_keys)
    return output[:, None]


def solution(mesh):
    in_specs = (
        P(("group", "sample"), None),
        P(),
        P("group", "sample", None),
        P("group"),
        P(None, "group", "sample", None),
    )
    out_specs = P(None, "group", "sample", None)
    return jax.shard_map(shards, mesh=mesh, in_specs=in_specs, out_specs=out_specs, check_vma=False)
```
